256 devices in a mesh: end: 2 (over z_lo), slab: 128 (over y, x, z_hi, core).
Axes of the slice: x: 4, y: 4, z: 8 (z_hi: 4, z_lo: 2; z = z_hi * 2 + z_lo), core: 2. Of those that a mesh axis runs over, the one named last changes fastest.
Arguments:
- w_field: float32 [1024, 128, 256], P('slab'), may hold values from -4 to 4
- psi_init: float32 [1024, 128, 256], P('slab'), may hold values from -3 to 3
- start_field: float32 [2, 1024, 128, 256], P('end', 'slab'), may hold values from 0.25 to 8, as said below
- charges: int32 [5], replicated, may hold values from -1 to 1
Outputs:
- density: float32 [1024, 128, 256], P('slab', 'end')
- potential: float32 [1024, 128, 256], P('slab', 'end')
The draws below stay inside these ranges and needn't reach their ends.
Inputs may be any that keep to these rules, and one draw needn't show every extreme that they name: `start_field`: positive entries.
All inputs are finite; a program needn't handle non-finite values.
Results may differ from the reference program's by a relative error of at most 0.0003.
The reference program's roundings to bfloat16 on the way count: a program that leaves them out, or rounds other values in their place, can miss the bound.
Values may be sent and summed in bfloat16 or wider, within the bound.
No kernel may reach another device: no remote copies, remote signals or barrier semaphores. Data moves between devices by JAX's collectives and lax.ppermute only.
A program may use at most 64 MiB of HBM per device.

```python
import jax
import jax.numpy as jnp
from jax import lax

NY = 128
NZ = 256
NS = 4
SWEEPS = 2
NX = 1024


def draw_start_field(key, part):
    position = jnp.arange(NX, dtype=jnp.float32) / (NX - 1)
    base = jax.random.uniform(key, (2, NX, NY, NZ), jnp.float32, 0.5, 1.5)
    ramp = 1.0 + 2.0 * position
    return base * ramp[None, :, None, None]


def set_ends(drawn, key, low, largest):
    longest = drawn.shape.index(max(drawn.shape))
    spots = []
    for shift in (0, 1):
        where = [jax.random.randint(jax.random.fold_in(key, axis), (), 0, length) for axis, length in enumerate(drawn.shape)]
        where[longest] = (where[longest] + shift) % drawn.shape[longest]
        spots.append(tuple(where))
    return drawn.at[spots[0]].set(low).at[spots[1]].set(largest)


def levels(own_key, shape, split, least, top_value):
    factor_of = 1.0
    for dim, parts in split:
        heights = jax.random.uniform(jax.random.fold_in(jax.random.fold_in(own_key, 6), dim), (parts,), jnp.float32, least / len(split), top_value / len(split))
        factor_of = factor_of * jnp.repeat(jnp.exp(heights), shape[dim] // parts).reshape((-1,) + (1,) * (len(shape) - 1 - dim))
    return factor_of


def noise(rng, dims, deviation, bound, pieces=(), kind=jnp.bfloat16):
    factor_of = levels(rng, dims, pieces, -0.22, 0.18) if pieces else 1.0
    entries = jax.random.normal(rng, dims, jnp.float32) * deviation * factor_of
    return jnp.minimum(jnp.maximum(entries, -bound), bound).astype(kind)


def setup_inputs(seed: int = 0) -> dict:
    splits = jax.random.split(jax.random.key(seed), 5)
    w_field = noise(splits[0], (NX, NY, NZ), 1.0, 4.0, ((0, 128),), jnp.float32)
    psi_init = noise(splits[1], (NX, NY, NZ), 0.5, 3.0, ((0, 128),), jnp.float32)
    start_field = draw_start_field(jax.random.fold_in(splits[4], 71), 0)
    charges = set_ends(jax.random.randint(splits[3], (NS + 1,), -1, 2), jax.random.fold_in(splits[3], 1), -1, 1).astype(jnp.int32)
    return dict(w_field=w_field, psi_init=psi_init, start_field=start_field, charges=charges)


mobility = 0.15
screening = 1.0
crowding = 0.5


def neighbour_sum(field):
    total = jnp.roll(field, 1, 0) + jnp.roll(field, -1, 0)
    total = total + jnp.roll(field, 1, 1) + jnp.roll(field, -1, 1)
    return total + jnp.roll(field, 1, 2) + jnp.roll(field, -1, 2)


def ion_charge(value):
    return screening * jnp.sinh(value) / (1.0 + crowding * (jnp.cosh(value) - 1.0))


def reference(w_field, psi_init, start_field, charges):
    delta = 1.0 / NS
    valence = charges.astype(jnp.float32)

    def advance(field, contour):
        factor = jnp.exp(-0.5 * delta * (w_field + 0.5 * (valence[contour] + valence[contour + 1]) * psi_init))
        scaled = factor * field
        return factor * (scaled + mobility * (neighbour_sum(scaled) - 6.0 * scaled))

    def rounded(field):
        return lax.optimization_barrier(field.astype(jnp.bfloat16)).astype(jnp.float32)

    forward = [start_field[0]]
    for contour in range(NS):
        forward.append(advance(forward[-1], contour))
    conjugate = start_field[1]
    phi_raw = jnp.zeros(w_field.shape, jnp.float32)
    rho_raw = jnp.zeros(w_field.shape, jnp.float32)
    for contour in range(NS, -1, -1):
        if contour < NS:
            conjugate = advance(conjugate, contour)
        product = rounded(forward[contour]) * rounded(conjugate)
        weight = delta * (0.5 if contour in (0, NS) else 1.0)
        phi_raw = phi_raw + weight * product
        rho_raw = rho_raw + (weight * valence[contour]) * product
    total = jnp.mean(phi_raw)
    density = phi_raw / total
    charge = rho_raw / total
    potential = psi_init
    for sweep in range(SWEEPS):
        potential = (neighbour_sum(potential) + charge - ion_charge(potential) + screening * potential) / (6.0 + screening)
    return density, potential
```

```python
import functools

import jax
import jax.numpy as jnp
from jax import lax
from jax.experimental import pallas as pl
from jax.experimental.pallas import tpu as pltpu
from jax.sharding import PartitionSpec as P

NS = 4
DELTA = 1.0 / NS
MOBILITY = 0.15
HALO = 8
AXES = ("end", "slab")

VMEM = pl.BlockSpec(memory_space=pltpu.VMEM)
SMEM = pl.BlockSpec(memory_space=pltpu.SMEM)


def call(kernel, outs, args, specs, scratch=(), flops=1e6, name=None):
    moved = sum(a.size * a.dtype.itemsize for a in args) + sum(o.size * o.dtype.itemsize for o in outs)
    return pl.pallas_call(
        kernel,
        out_shape=tuple(outs),
        in_specs=specs,
        out_specs=tuple(VMEM for _ in outs),
        scratch_shapes=list(scratch),
        cost_estimate=pl.CostEstimate(flops=int(flops), bytes_accessed=int(moved), transcendentals=0),
        compiler_params=pltpu.CompilerParams(vmem_limit_bytes=32 * 1024 * 1024),
        name=name,
    )(*args)


def sds(shape, dtype=jnp.float32):
    return jax.ShapeDtypeStruct(shape, dtype)


def pick(plane_of, dst, half, height):
    rows = height // 2
    base = pl.multiple_of(rows * half, 8)
    before = pl.multiple_of((height - HALO) - rows * half, 8)
    after = pl.multiple_of(rows - rows * half, 8)
    dst(0, HALO, plane_of(before, HALO))
    dst(HALO, rows, plane_of(base, rows))
    dst(HALO + rows, HALO, plane_of(after, HALO))


def extract(src, index, out, half, height):
    def read(at, n):
        return src[index + (pl.ds(at, n), slice(None))]

    def write(at, n, value):
        out[index[-1], pl.ds(at, n), :] = value

    pick(read, write, half, height)


def slopes(charges, side):
    values = []
    for step in range(NS):
        at = jnp.where(side == 0, step, NS - 1 - step)
        values.append(0.5 * (charges[at].astype(jnp.float32) + charges[at + 1].astype(jnp.float32)))
    return values


def factor(w, psi, slope):
    return jnp.exp(-0.5 * DELTA * (w + slope * psi))


def nsum_plane(value):
    rows, lanes = value.shape
    total = pltpu.roll(value, 1, 0) + pltpu.roll(value, rows - 1, 0)
    return total + pltpu.roll(value, 1, 1) + pltpu.roll(value, lanes - 1, 1)


def advance(before, here, after, scale):
    total = before + after + nsum_plane(here)
    return scale * (here + MOBILITY * (total - 6.0 * here))


def give_kernel(start, out):
    side = lax.axis_index("end")
    for plane in range(start.shape[1]):
        extract(start, (0, plane), out, 1 - side, start.shape[2])


def own_kernel(charges, w, psi, start, w_out, psi_out, u_out, slice_out):
    side = lax.axis_index("end")
    slope = slopes(charges, side)
    height = w.shape[1]
    for plane in range(w.shape[0]):
        extract(w, (plane,), w_out, side, height)
        extract(psi, (plane,), psi_out, side, height)
        extract(start, (0, plane), u_out, side, height)
        value = u_out[plane]
        slice_out[plane] = value.astype(jnp.bfloat16)
        u_out[plane] = factor(w_out[plane], psi_out[plane], slope[0]) * value


def both_kernel(charges, got, w, psi, u_own, u_out, slice_out, pay_core, pay_chip):
    side = lax.axis_index("end")
    core = lax.rem(lax.axis_index("slab"), 2)
    slope = slopes(charges, side)
    planes = got.shape[0]
    for plane in range(planes):
        value = got[plane]
        slice_out[plane] = value.astype(jnp.bfloat16)
        u_out[plane] = factor(w[plane], psi[plane], slope[NS - 1]) * value
    first = jnp.where(core == 0, planes - 2, 0)
    second = planes - 2 - first
    for pay, at in ((pay_core, first), (pay_chip, second)):
        edge = jnp.where(at == 0, 0, planes - 1)
        for k in range(2):
            pay[k] = u_own[at + k]
            pay[2 + k] = u_out[at + k]
        pay[4] = w[edge]
        pay[5] = psi[edge]


def early_kernel(charges, u_own, u_other, w, psi, got_core, got_chip,
                 own_1, own_2, other_1, other_2, u_own_out, u_other_out, base, pay_core, pay_chip, held):
    side = lax.axis_index("end")
    core = lax.rem(lax.axis_index("slab"), 2)
    slope = slopes(charges, side)
    planes = w.shape[0]

    def halo(upper, k):
        if upper:
            return jnp.where(core == 0, got_core[k], got_chip[k])
        return jnp.where(core == 0, got_chip[k], got_core[k])

    def load(ref, offset, plane):
        if plane < 0:
            return halo(False, offset + plane + 2)
        if plane >= planes:
            return halo(True, offset + plane - planes)
        return ref[plane]

    def load_edge(ref, k, plane):
        if plane < 0:
            return halo(False, k)
        if plane >= planes:
            return halo(True, k)
        return ref[plane]

    chains = ((u_own, 0, own_1, own_2, u_own_out, (0, 1, 2)), (u_other, 2, other_1, other_2, u_other_out, (3, 2, 1)))
    for which, (u, offset, out_1, out_2, u_out, order) in enumerate(chains):
        for plane in range(-1, planes + 1):
            w_here, psi_here = load_edge(w, 4, plane), load_edge(psi, 5, plane)
            value = advance(load(u, offset, plane - 1), load(u, offset, plane), load(u, offset, plane + 1),
                            factor(w_here, psi_here, slope[order[0]]))
            if 0 <= plane < planes:
                out_1[plane] = value.astype(jnp.bfloat16)
            held[which, plane + 1] = factor(w_here, psi_here, slope[order[1]]) * value
        for plane in range(planes):
            value = advance(held[which, plane], held[which, plane + 1], held[which, plane + 2],
                            factor(w[plane], psi[plane], slope[order[1]]))
            out_2[plane] = value.astype(jnp.bfloat16)
            u_out[plane] = factor(w[plane], psi[plane], slope[order[2]]) * value
    first = jnp.where(core == 0, planes - 2, 0)
    second = planes - 2 - first
    for pay, at in ((pay_core, first), (pay_chip, second)):
        for k in range(2):
            pay[k] = u_own_out[at + k]
            pay[2 + k] = u_other_out[at + k]
    for plane in range(planes):
        here = psi[plane]
        total = load_edge(psi, 5, plane - 1) + load_edge(psi, 5, plane + 1) + nsum_plane(here)
        base[plane] = (total - 2.0 * jnp.tanh(0.5 * here) + here) / 7.0


def late_kernel(charges, u_own, u_other, w, psi, wide_core, wide_chip, got_core, got_chip,
                own_0, own_1, own_2, other_0, other_1, other_2, base,
                phi, rho, sums, pay_core, pay_chip, held, last):
    side = lax.axis_index("end")
    core = lax.rem(lax.axis_index("slab"), 2)
    slope = slopes(charges, side)
    planes, _, lanes = w.shape
    rows = phi.shape[1]

    def halo(core_ref, chip_ref, upper, k):
        if upper:
            return jnp.where(core == 0, core_ref[k], chip_ref[k])
        return jnp.where(core == 0, chip_ref[k], core_ref[k])

    def load(ref, offset, plane):
        if plane < 0:
            return halo(got_core, got_chip, False, offset + plane + 2)
        if plane >= planes:
            return halo(got_core, got_chip, True, offset + plane - planes)
        return ref[plane]

    def load_edge(ref, k, plane):
        if plane < 0:
            return halo(wide_core, wide_chip, False, k)
        if plane >= planes:
            return halo(wide_core, wide_chip, True, k)
        return ref[plane]

    chains = ((u_own, 0, (2, 3)), (u_other, 2, (1, 0)))
    for which, (u, offset, order) in enumerate(chains):
        for plane in range(-1, planes + 1):
            w_here, psi_here = load_edge(w, 4, plane), load_edge(psi, 5, plane)
            value = advance(load(u, offset, plane - 1), load(u, offset, plane), load(u, offset, plane + 1),
                            factor(w_here, psi_here, slope[order[0]]))
            if 0 <= plane < planes:
                last[which, 0, plane] = value.astype(jnp.bfloat16)
            held[which, plane + 1] = factor(w_here, psi_here, slope[order[1]]) * value
        for plane in range(planes):
            value = advance(held[which, plane], held[which, plane + 1], held[which, plane + 2],
                            factor(w[plane], psi[plane], slope[order[1]]))
            last[which, 1, plane] = value.astype(jnp.bfloat16)
    weights = [DELTA * (0.5 if k in (0, NS) else 1.0) for k in range(NS + 1)]
    valence = [charges[jnp.where(side == 0, k, NS - k)].astype(jnp.float32) for k in range(NS + 1)]
    partial = jnp.zeros((8, lanes), jnp.float32)
    for plane in range(planes):
        own = (own_0[plane], own_1[plane], own_2[plane], last[0, 0, plane], last[0, 1, plane])
        other = (other_0[plane], other_1[plane], other_2[plane], last[1, 0, plane], last[1, 1, plane])
        phi_here = rho_here = None
        for k in range(NS + 1):
            product = own[k].astype(jnp.float32) * other[NS - k].astype(jnp.float32)
            if k == 0:
                phi_here, rho_here = weights[k] * product, (weights[k] * valence[k]) * product
            else:
                phi_here = phi_here + weights[k] * product
                rho_here = rho_here + (weights[k] * valence[k]) * product
        kept = phi_here[HALO:HALO + rows]
        phi[plane] = kept
        rho[plane] = rho_here
        for at in range(0, rows, 8):
            partial = partial + kept[at:at + 8]
    row = jnp.sum(partial, 0, keepdims=True)
    row = row[:, :lanes // 2] + row[:, lanes // 2:]
    sums[...] = jnp.broadcast_to(row, sums.shape)
    first = jnp.where(core == 0, planes - 1, 0)
    second = planes - 1 - first
    for pay, at in ((pay_core, first), (pay_chip, second)):
        pay[0] = base[at]
        pay[1] = rho[at]


def end_kernel(cells, phi, rho, base, got_core, got_chip, sums, density, potential, held):
    core = lax.rem(lax.axis_index("slab"), 2)
    planes = phi.shape[0]
    rows = phi.shape[1]
    inverse = cells / jnp.sum(sums[...], keepdims=True)

    def halo(upper, k):
        if upper:
            return jnp.where(core == 0, got_core[k], got_chip[k])
        return jnp.where(core == 0, got_chip[k], got_core[k])

    share = inverse / 7.0
    held[0] = halo(False, 0) + halo(False, 1) * share
    held[planes + 1] = halo(True, 0) + halo(True, 1) * share
    for plane in range(planes):
        held[plane + 1] = base[plane] + rho[plane] * share
    for plane in range(planes):
        density[plane] = phi[plane] * inverse
        here = held[plane + 1]
        total = held[plane] + held[plane + 2] + nsum_plane(here)
        value = (total + rho[plane] * inverse - 2.0 * jnp.tanh(0.5 * here) + here) / 7.0
        potential[plane] = value[HALO:HALO + rows]


def body(w_field, psi_init, start_field, charges):
    ends, slabs = lax.axis_size("end"), lax.axis_size("slab")
    count = ends * slabs
    planes, height, lanes = w_field.shape
    rows = height // 2
    wide = rows + 2 * HALO
    swap = [(i, (i + slabs) % count) for i in range(count)]
    by_core = [(i, i ^ 1) for i in range(count)]
    by_chip = []
    for i in range(count):
        at, tile = divmod(i, slabs)
        by_chip.append((i, at * slabs + (tile + (1 if tile % 2 else -1)) % slabs))
    tile = sds((planes, wide, lanes))
    narrow = sds((planes, wide, lanes), jnp.bfloat16)

    (given,) = call(give_kernel, [tile], [start_field], [VMEM], name="give")
    got = lax.ppermute(given, AXES, swap)
    w, psi, u_own, own_0 = call(
        own_kernel, [tile, tile, tile, narrow], [charges, w_field, psi_init, start_field], [SMEM] + [VMEM] * 3,
        name="own")
    u_other, other_0, pay_core, pay_chip = call(
        both_kernel, [tile, narrow, sds((6, wide, lanes)), sds((6, wide, lanes))],
        [charges, got, w, psi, u_own], [SMEM] + [VMEM] * 4, name="both")
    wide_chip = lax.ppermute(pay_chip, AXES, by_chip)
    wide_core = lax.ppermute(pay_core, AXES, by_core)
    held = pltpu.VMEM((2, planes + 2, wide, lanes), jnp.float32)
    own_1, own_2, other_1, other_2, u_own, u_other, base, pay_core, pay_chip = call(
        early_kernel, [narrow] * 4 + [tile] * 3 + [sds((4, wide, lanes))] * 2,
        [charges, u_own, u_other, w, psi, wide_core, wide_chip], [SMEM] + [VMEM] * 6, [held], name="early")
    got_chip = lax.ppermute(pay_chip, AXES, by_chip)
    got_core = lax.ppermute(pay_core, AXES, by_core)
    phi, rho, sums, pay_core, pay_chip = call(
        late_kernel,
        [sds((planes, rows, lanes)), tile, sds((count, lanes // 2)), sds((2, wide, lanes)), sds((2, wide, lanes))],
        [charges, u_own, u_other, w, psi, wide_core, wide_chip, got_core, got_chip,
         own_0, own_1, own_2, other_0, other_1, other_2, base],
        [SMEM] + [VMEM] * 15, [held, pltpu.VMEM((2, 2, planes, wide, lanes), jnp.bfloat16)], name="late")
    got_chip = lax.ppermute(pay_chip, AXES, by_chip)
    got_core = lax.ppermute(pay_core, AXES, by_core)
    sums = lax.all_to_all(sums, AXES, 0, 0, tiled=True)
    cells = float(slabs * planes * height * lanes)
    density, potential = call(
        functools.partial(end_kernel, cells), [sds((planes, rows, lanes))] * 2,
        [phi, rho, base, got_core, got_chip, sums], [VMEM] * 6,
        [pltpu.VMEM((planes + 2, wide, lanes), jnp.float32)], name="finish")
    return density, potential


def solution(mesh):
    in_specs = (P("slab", None, None), P("slab", None, None), P("end", "slab", None, None), P())
    out_specs = (P("slab", "end", None), P("slab", "end", None))
    return jax.shard_map(body, mesh=mesh, in_specs=in_specs, out_specs=out_specs, check_vma=False)
```

```python
import functools

import jax
import jax.numpy as jnp
from jax import lax
from jax.experimental import pallas as pl
from jax.experimental.pallas import tpu as pltpu
from jax.sharding import PartitionSpec as P

NS = 4
DELTA = 1.0 / NS
MOBILITY = 0.15
HALO = 8
AXES = ("end", "slab")

VMEM = pl.BlockSpec(memory_space=pltpu.VMEM)
ANY = pl.BlockSpec(memory_space=pl.ANY)
SMEM = pl.BlockSpec(memory_space=pltpu.SMEM)


def call(kernel, outs, args, specs, scratch=(), flops=1e6, name=None):
    moved = sum(a.size * a.dtype.itemsize for a in args) + sum(o.size * o.dtype.itemsize for o in outs)
    return pl.pallas_call(
        kernel,
        out_shape=tuple(outs),
        in_specs=specs,
        out_specs=tuple(VMEM for _ in outs),
        scratch_shapes=list(scratch),
        cost_estimate=pl.CostEstimate(flops=int(flops), bytes_accessed=int(moved), transcendentals=0),
        compiler_params=pltpu.CompilerParams(vmem_limit_bytes=32 * 1024 * 1024),
        name=name,
    )(*args)


def sds(shape, dtype=jnp.float32):
    return jax.ShapeDtypeStruct(shape, dtype)


def pick(plane_of, dst, half, height):
    rows = height // 2
    base = pl.multiple_of(rows * half, 8)
    before = pl.multiple_of((height - HALO) - rows * half, 8)
    after = pl.multiple_of(rows - rows * half, 8)
    dst(0, HALO, plane_of(before, HALO))
    dst(HALO, rows, plane_of(base, rows))
    dst(HALO + rows, HALO, plane_of(after, HALO))


def extract(src, index, out, half, height):
    def read(at, n):
        return src[index + (pl.ds(at, n), slice(None))]

    def write(at, n, value):
        out[index[-1], pl.ds(at, n), :] = value

    pick(read, write, half, height)


def slopes(charges, side):
    values = []
    for step in range(NS):
        at = jnp.where(side == 0, step, NS - 1 - step)
        values.append(0.5 * (charges[at].astype(jnp.float32) + charges[at + 1].astype(jnp.float32)))
    return values


def factor(w, psi, slope):
    return jnp.exp(-0.5 * DELTA * (w + slope * psi))


def nsum_plane(value):
    rows, lanes = value.shape
    total = pltpu.roll(value, 1, 0) + pltpu.roll(value, rows - 1, 0)
    return total + pltpu.roll(value, 1, 1) + pltpu.roll(value, lanes - 1, 1)


def advance(before, here, after, scale):
    total = before + after + nsum_plane(here)
    return scale * (here + MOBILITY * (total - 6.0 * here))


def edges(core, planes, width):
    to_core = jnp.where(core == 0, planes - width, 0)
    return to_core, planes - width - to_core


def place():
    return lax.axis_index("end"), lax.rem(lax.axis_index("slab"), 2)


def halo(core, from_core, from_chip, upper, k):
    if upper:
        return jnp.where(core == 0, from_core[k], from_chip[k])
    return jnp.where(core == 0, from_chip[k], from_core[k])


def around(core, ref, from_core, from_chip, base, width):
    planes = ref.shape[0]

    def load(plane):
        if plane < 0:
            return halo(core, from_core, from_chip, False, base + plane + width)
        if plane >= planes:
            return halo(core, from_core, from_chip, True, base + plane - planes)
        return ref[plane]

    return load


def give_kernel(start, out):
    side = lax.axis_index("end")
    for plane in range(start.shape[1]):
        extract(start, (0, plane), out, 1 - side, start.shape[2])


def own_kernel(charges, w, psi, start, w_out, psi_out, u_out, slice_out, pay_core, pay_chip):
    side, core = place()
    slope = slopes(charges, side)
    planes, height = w.shape[0], w.shape[1]
    for plane in range(planes):
        extract(w, (plane,), w_out, side, height)
        extract(psi, (plane,), psi_out, side, height)
        extract(start, (0, plane), u_out, side, height)
        value = u_out[plane]
        slice_out[plane] = value.astype(jnp.bfloat16)
        u_out[plane] = factor(w_out[plane], psi_out[plane], slope[0]) * value
    for pay, at, edge in zip((pay_core, pay_chip), edges(core, planes, 2), edges(core, planes, 1)):
        pay[0] = u_out[at]
        pay[1] = u_out[at + 1]
        pay[2] = w_out[edge]
        pay[3] = psi_out[edge]


def other_kernel(charges, got, w, psi, u_out, slice_out, pay_core, pay_chip):
    side, core = place()
    slope = slopes(charges, side)
    planes = got.shape[0]
    for plane in range(planes):
        value = got[plane]
        slice_out[plane] = value.astype(jnp.bfloat16)
        u_out[plane] = factor(w[plane], psi[plane], slope[NS - 1]) * value
    for pay, at in zip((pay_core, pay_chip), edges(core, planes, 2)):
        pay[0] = u_out[at]
        pay[1] = u_out[at + 1]


def two_steps(load_u, load_w, load_psi, planes, slope, order, held, out_first, out_second, u_out):
    for plane in range(-1, planes + 1):
        w_here, psi_here = load_w(plane), load_psi(plane)
        value = advance(load_u(plane - 1), load_u(plane), load_u(plane + 1), factor(w_here, psi_here, slope[order[0]]))
        if 0 <= plane < planes:
            out_first[plane] = value.astype(jnp.bfloat16)
        held[plane + 1] = factor(w_here, psi_here, slope[order[1]]) * value
    for plane in range(planes):
        w_here, psi_here = load_w(plane), load_psi(plane)
        value = advance(held[plane], held[plane + 1], held[plane + 2], factor(w_here, psi_here, slope[order[1]]))
        out_second[plane] = value.astype(jnp.bfloat16)
        if u_out is not None:
            u_out[plane] = factor(w_here, psi_here, slope[order[2]]) * value


def own_early_kernel(charges, u, w, psi, wide_core, wide_chip, after, out_1, out_2, u_out, base, pay_core, pay_chip, held):
    del after
    side, core = place()
    planes = w.shape[0]
    load_psi = around(core, psi, wide_core, wide_chip, 3, 1)
    two_steps(around(core, u, wide_core, wide_chip, 0, 2), around(core, w, wide_core, wide_chip, 2, 1), load_psi,
              planes, slopes(charges, side), (0, 1, 2), held, out_1, out_2, u_out)
    for plane in range(planes):
        here = psi[plane]
        total = load_psi(plane - 1) + load_psi(plane + 1) + nsum_plane(here)
        base[plane] = (total - 2.0 * jnp.tanh(0.5 * here) + here) / 7.0
    for pay, at, edge in zip((pay_core, pay_chip), edges(core, planes, 2), edges(core, planes, 1)):
        pay[0] = u_out[at]
        pay[1] = u_out[at + 1]
        pay[2] = base[edge]


def other_early_kernel(charges, u, w, psi, wide_core, wide_chip, got_core, got_chip,
                       out_1, out_2, u_out, pay_core, pay_chip, held):
    side, core = place()
    planes = w.shape[0]
    two_steps(around(core, u, got_core, got_chip, 0, 2), around(core, w, wide_core, wide_chip, 2, 1),
              around(core, psi, wide_core, wide_chip, 3, 1),
              planes, slopes(charges, side), (3, 2, 1), held, out_1, out_2, u_out)
    for pay, at in zip((pay_core, pay_chip), edges(core, planes, 2)):
        pay[0] = u_out[at]
        pay[1] = u_out[at + 1]


def own_late_kernel(charges, u, w, psi, wide_core, wide_chip, got_core, got_chip, after, out_3, out_4, held):
    del after
    side, core = place()
    two_steps(around(core, u, got_core, got_chip, 0, 2), around(core, w, wide_core, wide_chip, 2, 1),
              around(core, psi, wide_core, wide_chip, 3, 1),
              w.shape[0], slopes(charges, side), (2, 3), held, out_3, out_4, None)


def products(own, other, charges, side):
    phi = rho = None
    for k in range(NS + 1):
        weight = DELTA * (0.5 if k in (0, NS) else 1.0)
        valence = charges[jnp.where(side == 0, k, NS - k)].astype(jnp.float32)
        product = own[k].astype(jnp.float32) * other[NS - k].astype(jnp.float32)
        if phi is None:
            phi, rho = weight * product, (weight * valence) * product
        else:
            phi, rho = phi + weight * product, rho + (weight * valence) * product
    return phi, rho


def rim_kernel(charges, u, w, psi, wide_core, wide_chip, got_core, got_chip,
               own_0, own_1, own_2, own_3, own_4, other_0, other_1, other_2,
               u_out, other_3, phi, rho, pay_core, pay_chip, held):
    side, core = place()
    slope = slopes(charges, side)
    planes = w.shape[0]
    load_u = around(core, u, got_core, got_chip, 0, 2)
    load_w = around(core, w, wide_core, wide_chip, 2, 1)
    load_psi = around(core, psi, wide_core, wide_chip, 3, 1)
    for end, (spot, steps) in enumerate(((0, (-1, 0, 1)), (planes - 1, (planes - 2, planes - 1, planes)))):
        for at, plane in enumerate(steps):
            w_here, psi_here = load_w(plane), load_psi(plane)
            value = advance(load_u(plane - 1), load_u(plane), load_u(plane + 1), factor(w_here, psi_here, slope[1]))
            if 0 <= plane < planes:
                other_3[plane] = value.astype(jnp.bfloat16)
            value = factor(w_here, psi_here, slope[0]) * value
            held[at] = value
            if 0 <= plane < planes:
                u_out[plane] = value
        last = advance(held[0], held[1], held[2], factor(w[spot], psi[spot], slope[0])).astype(jnp.bfloat16)
        phi[end], rho[end] = products(
            (own_0[spot], own_1[spot], own_2[spot], own_3[spot], own_4[spot]),
            (other_0[spot], other_1[spot], other_2[spot], other_3[spot], last), charges, side)
    for pay, at in zip((pay_core, pay_chip), edges(core, 2, 1)):
        pay[0] = rho[at]


def inner_kernel(charges, u, w, psi, u_rim, rim_3, phi_rim, rho_rim,
                 own_0, own_1, own_2, own_3, own_4, other_0, other_1, other_2,
                 phi, rho, sums, held, other_3):
    side = lax.axis_index("end")
    slope = slopes(charges, side)
    planes, _, lanes = w.shape
    rows = phi.shape[1]
    for plane in range(2, planes - 2):
        value = advance(u[plane - 1], u[plane], u[plane + 1], factor(w[plane], psi[plane], slope[1]))
        other_3[plane] = value.astype(jnp.bfloat16)
        held[plane] = factor(w[plane], psi[plane], slope[0]) * value
    partial = jnp.zeros((8, lanes), jnp.float32)
    inside = range(2, planes - 2)

    def at(plane):
        return held[plane] if plane in inside else u_rim[plane]

    for plane in range(planes):
        if plane in (0, planes - 1):
            end = 0 if plane == 0 else 1
            phi_here, rho_here = phi_rim[end], rho_rim[end]
        else:
            last = advance(at(plane - 1), at(plane), at(plane + 1), factor(w[plane], psi[plane], slope[0]))
            third = other_3[plane] if plane in inside else rim_3[plane]
            phi_here, rho_here = products(
                (own_0[plane], own_1[plane], own_2[plane], own_3[plane], own_4[plane]),
                (other_0[plane], other_1[plane], other_2[plane], third, last.astype(jnp.bfloat16)), charges, side)
        kept = phi_here[HALO:HALO + rows]
        phi[plane] = kept
        rho[plane] = rho_here
        for row in range(0, rows, 8):
            partial = partial + kept[row:row + 8]
    row = jnp.sum(partial, 0, keepdims=True)
    row = row[:, :lanes // 2] + row[:, lanes // 2:]
    sums[...] = jnp.broadcast_to(row, sums.shape)


def end_kernel(cells, phi, rho, base, base_core, base_chip, got_core, got_chip, sums, density, potential, held):
    _, core = place()
    planes, rows, _ = phi.shape
    inverse = cells / jnp.sum(sums[...], keepdims=True)
    share = inverse / 7.0
    load_base = around(core, base, base_core, base_chip, 2, 1)
    load_rho = around(core, rho, got_core, got_chip, 0, 1)
    for plane in range(-1, planes + 1):
        held[plane + 1] = load_base(plane) + load_rho(plane) * share
    for plane in range(planes):
        density[plane] = phi[plane] * inverse
        here = held[plane + 1]
        total = held[plane] + held[plane + 2] + nsum_plane(here)
        value = (total + rho[plane] * inverse - 2.0 * jnp.tanh(0.5 * here) + here) / 7.0
        potential[plane] = value[HALO:HALO + rows]


def body(w_field, psi_init, start_field, charges):
    ends, slabs = lax.axis_size("end"), lax.axis_size("slab")
    count = ends * slabs
    planes, height, lanes = w_field.shape
    rows = height // 2
    wide = rows + 2 * HALO
    swap = [(i, (i + slabs) % count) for i in range(count)]
    by_core = [(i, i ^ 1) for i in range(count)]
    by_chip = []
    for i in range(count):
        at, tile = divmod(i, slabs)
        by_chip.append((i, at * slabs + (tile + (1 if tile % 2 else -1)) % slabs))

    def exchange(pay_core, pay_chip):
        return lax.ppermute(pay_core, AXES, by_core), lax.ppermute(pay_chip, AXES, by_chip)

    tile = sds((planes, wide, lanes))
    narrow = sds((planes, wide, lanes), jnp.bfloat16)
    held = pltpu.VMEM((planes + 2, wide, lanes), jnp.float32)

    def pays(k):
        return [sds((k, wide, lanes))] * 2

    (given,) = call(give_kernel, [tile], [start_field], [VMEM], name="give")
    got = lax.ppermute(given, AXES, swap)
    w, psi, u_own, own_0, *pay = call(
        own_kernel, [tile, tile, tile, narrow] + pays(4), [charges, w_field, psi_init, start_field],
        [SMEM] + [VMEM] * 3, name="own")
    fields = exchange(*pay)
    u_other, other_0, *pay = call(
        other_kernel, [tile, narrow] + pays(2), [charges, got, w, psi], [SMEM] + [VMEM] * 3, name="other")
    early = exchange(*pay)
    own_1, own_2, u_own, base, *pay = call(
        own_early_kernel, [narrow, narrow, tile, tile] + pays(3), [charges, u_own, w, psi, *fields, u_other],
        [SMEM] + [VMEM] * 5 + [ANY], [held], name="own_early")
    own_edge = exchange(*pay)
    other_1, other_2, u_other, *pay = call(
        other_early_kernel, [narrow, narrow, tile] + pays(2), [charges, u_other, w, psi, *fields, *early],
        [SMEM] + [VMEM] * 7, [held], name="other_early")
    other_edge = exchange(*pay)
    own_3, own_4 = call(
        own_late_kernel, [narrow, narrow], [charges, u_own, w, psi, *fields, *own_edge, u_other],
        [SMEM] + [VMEM] * 7 + [ANY], [held], name="own_late")
    slices = [own_0, own_1, own_2, own_3, own_4, other_0, other_1, other_2]
    u_rim, rim_3, phi_rim, rho_rim, *pay = call(
        rim_kernel, [tile, narrow, sds((2, wide, lanes)), sds((2, wide, lanes))] + pays(1),
        [charges, u_other, w, psi, *fields, *other_edge, *slices], [SMEM] + [VMEM] * 15,
        [pltpu.VMEM((3, wide, lanes), jnp.float32)], name="rim")
    rho_edge = exchange(*pay)
    phi, rho, sums = call(
        inner_kernel, [sds((planes, rows, lanes)), tile, sds((count, lanes // 2))],
        [charges, u_other, w, psi, u_rim, rim_3, phi_rim, rho_rim, *slices], [SMEM] + [VMEM] * 15,
        [pltpu.VMEM((planes, wide, lanes), jnp.float32), pltpu.VMEM((planes, wide, lanes), jnp.bfloat16)], name="inner")
    sums, *rho_edge = lax.optimization_barrier((sums, *rho_edge))
    sums = lax.all_to_all(sums, AXES, 0, 0, tiled=True)
    cells = float(slabs * planes * height * lanes)
    return tuple(call(
        functools.partial(end_kernel, cells), [sds((planes, rows, lanes))] * 2,
        [phi, rho, base, *own_edge, *rho_edge, sums], [VMEM] * 8, [held], name="finish"))


def solution(mesh):
    in_specs = (P("slab", None, None), P("slab", None, None), P("end", "slab", None, None), P())
    out_specs = (P("slab", "end", None), P("slab", "end", None))
    return jax.shard_map(body, mesh=mesh, in_specs=in_specs, out_specs=out_specs, check_vma=False)
```

```python
import functools

import jax
import jax.numpy as jnp
from jax import lax
from jax.experimental import pallas as pl
from jax.experimental.pallas import tpu as pltpu
from jax.sharding import PartitionSpec as P

NS = 4
DELTA = 1.0 / NS
MOBILITY = 0.15
HALO = 8
AXES = ("end", "slab")

VMEM = pl.BlockSpec(memory_space=pltpu.VMEM)
ANY = pl.BlockSpec(memory_space=pl.ANY)
SMEM = pl.BlockSpec(memory_space=pltpu.SMEM)


def call(kernel, outs, args, specs, scratch=(), flops=2e9, name=None):
    moved = sum(a.size * a.dtype.itemsize for a in args) + sum(o.size * o.dtype.itemsize for o in outs)
    return pl.pallas_call(
        kernel,
        out_shape=tuple(outs),
        in_specs=specs,
        out_specs=tuple(VMEM for _ in outs),
        scratch_shapes=list(scratch),
        cost_estimate=pl.CostEstimate(flops=int(flops), bytes_accessed=int(moved), transcendentals=0),
        compiler_params=pltpu.CompilerParams(vmem_limit_bytes=16 * 1024 * 1024),
        name=name,
    )(*args)


def sds(shape, dtype=jnp.float32):
    return jax.ShapeDtypeStruct(shape, dtype)


def pick(plane_of, dst, half, height):
    rows = height // 2
    base = pl.multiple_of(rows * half, 8)
    before = pl.multiple_of((height - HALO) - rows * half, 8)
    after = pl.multiple_of(rows - rows * half, 8)
    dst(0, HALO, plane_of(before, HALO))
    dst(HALO, rows, plane_of(base, rows))
    dst(HALO + rows, HALO, plane_of(after, HALO))


def extract(src, index, out, half, height):
    def read(at, n):
        return src[index + (pl.ds(at, n), slice(None))]

    def write(at, n, value):
        out[index[-1], pl.ds(at, n), :] = value

    pick(read, write, half, height)


def slopes(charges, side):
    values = []
    for step in range(NS):
        at = jnp.where(side == 0, step, NS - 1 - step)
        values.append(0.5 * (charges[at].astype(jnp.float32) + charges[at + 1].astype(jnp.float32)))
    return values


def factor(w, psi, slope):
    return jnp.exp(-0.5 * DELTA * (w + slope * psi))


def nsum_plane(value):
    rows, lanes = value.shape
    total = pltpu.roll(value, 1, 0) + pltpu.roll(value, rows - 1, 0)
    return total + pltpu.roll(value, 1, 1) + pltpu.roll(value, lanes - 1, 1)


def advance(before, here, after, scale):
    total = before + after + nsum_plane(here)
    return scale * (here + MOBILITY * (total - 6.0 * here))


def edges(core, planes, width):
    to_core = jnp.where(core == 0, planes - width, 0)
    return to_core, planes - width - to_core


def place():
    return lax.axis_index("end"), lax.rem(lax.axis_index("slab"), 2)


def around(core, load_inside, planes, from_core, from_chip, base, width):
    def load(plane):
        if plane < 0:
            k = base + plane + width
            return jnp.where(core == 0, from_chip[k], from_core[k])
        if plane >= planes:
            k = base + plane - planes
            return jnp.where(core == 0, from_core[k], from_chip[k])
        return load_inside(plane)

    return load


def fields_around(core, w, psi, fields):
    planes = w.shape[0]
    return (around(core, lambda p: w[p], planes, *fields, 2, 2), around(core, lambda p: psi[p], planes, *fields, 4, 2))


def split(planes):
    return [0, 1, planes - 2, planes - 1], list(range(2, planes - 2))


def give_kernel(which, start, *rest):
    out = rest[-1]
    side = lax.axis_index("end")
    for at, plane in enumerate(which):
        def read(row, n):
            return start[0, plane, pl.ds(row, n), :]

        def write(row, n, value):
            out[at, pl.ds(row, n), :] = value

        pick(read, write, 1 - side, start.shape[2])


def own_kernel(charges, w, psi, start, after, w_out, psi_out, u_out, slice_out, pay_core, pay_chip):
    del after
    side, core = place()
    slope = slopes(charges, side)
    planes, height = w.shape[0], w.shape[1]
    for plane in range(planes):
        extract(w, (plane,), w_out, side, height)
        extract(psi, (plane,), psi_out, side, height)
        extract(start, (0, plane), u_out, side, height)
        value = u_out[plane]
        slice_out[plane] = value.astype(jnp.bfloat16)
        u_out[plane] = factor(w_out[plane], psi_out[plane], slope[0]) * value
    for pay, at in zip((pay_core, pay_chip), edges(core, planes, 2)):
        for k in range(2):
            pay[k] = u_out[at + k]
            pay[2 + k] = w_out[at + k]
            pay[4 + k] = psi_out[at + k]


def other_kernel(charges, got_rim, w, psi, u_rim, pay_core, pay_chip):
    side, core = place()
    slope = slopes(charges, side)
    rim, _ = split(w.shape[0])
    for at, plane in enumerate(rim):
        u_rim[at] = factor(w[plane], psi[plane], slope[NS - 1]) * got_rim[at]
    for pay, at in zip((pay_core, pay_chip), edges(core, 4, 2)):
        for k in range(2):
            pay[k] = u_rim[at + k]


def early_steps(load_u, load_w, load_psi, planes, slope, order, held, out_first, out_second, u_out, pays, core):
    for plane in range(-1, planes + 1):
        w_here, psi_here = load_w(plane), load_psi(plane)
        value = advance(load_u(plane - 1), load_u(plane), load_u(plane + 1), factor(w_here, psi_here, slope[order[0]]))
        out_first[plane + 1] = value.astype(jnp.bfloat16)
        held[plane + 1] = factor(w_here, psi_here, slope[order[1]]) * value
    for plane in range(planes):
        w_here, psi_here = load_w(plane), load_psi(plane)
        value = advance(held[plane], held[plane + 1], held[plane + 2], factor(w_here, psi_here, slope[order[1]]))
        out_second[plane] = value.astype(jnp.bfloat16)
        u_out[plane] = factor(w_here, psi_here, slope[order[2]]) * value
    for pay, at in zip(pays, edges(core, planes, 3)):
        for k in range(3):
            pay[k] = u_out[at + k]


def own_early_kernel(charges, u, w, psi, wide_core, wide_chip, after, out_1, out_2, u_out, pay_core, pay_chip, held):
    del after
    side, core = place()
    planes = w.shape[0]
    fields = (wide_core, wide_chip)
    early_steps(around(core, lambda p: u[p], planes, *fields, 0, 2), *fields_around(core, w, psi, fields), planes,
                slopes(charges, side), (0, 1, 2), held, out_1, out_2, u_out, (pay_core, pay_chip), core)


def other_early_kernel(charges, u_rim, got_mid, w, psi, wide_core, wide_chip, got_core, got_chip,
                       out_1, out_2, u_out, pay_core, pay_chip, held, u_mid):
    side, core = place()
    slope = slopes(charges, side)
    planes = w.shape[0]
    rim, middle = split(planes)
    for at, plane in enumerate(middle):
        u_mid[at] = factor(w[plane], psi[plane], slope[NS - 1]) * got_mid[at]

    def inside(plane):
        return u_rim[rim.index(plane)] if plane in rim else u_mid[middle.index(plane)]

    early_steps(around(core, inside, planes, got_core, got_chip, 0, 2),
                *fields_around(core, w, psi, (wide_core, wide_chip)), planes,
                slope, (3, 2, 1), held, out_1, out_2, u_out, (pay_core, pay_chip), core)


def late_steps(load_u, load_w, load_psi, planes, slope, order, held, out_third, emit_last):
    for plane in range(-2, planes + 2):
        w_here, psi_here = load_w(plane), load_psi(plane)
        value = advance(load_u(plane - 1), load_u(plane), load_u(plane + 1), factor(w_here, psi_here, slope[order[0]]))
        if -1 <= plane <= planes:
            out_third[plane + 1] = value.astype(jnp.bfloat16)
        held[plane + 2] = factor(w_here, psi_here, slope[order[1]]) * value
    for plane in range(-1, planes + 1):
        value = advance(held[plane + 1], held[plane + 2], held[plane + 3],
                        factor(load_w(plane), load_psi(plane), slope[order[1]]))
        emit_last(plane, value.astype(jnp.bfloat16))


def sweep_base(here, before, after):
    total = before + after + nsum_plane(here)
    return (total - 2.0 * jnp.tanh(0.5 * here) + here) / 7.0


def own_late_kernel(charges, u, w, psi, wide_core, wide_chip, got_core, got_chip, after, out_3, out_4, base, held):
    del after
    side, core = place()
    planes = w.shape[0]
    load_w, load_psi = fields_around(core, w, psi, (wide_core, wide_chip))

    def emit(plane, value):
        out_4[plane + 1] = value

    late_steps(around(core, lambda p: u[p], planes, got_core, got_chip, 0, 3), load_w, load_psi,
               planes, slopes(charges, side), (2, 3), held, out_3, emit)
    for plane in range(planes):
        base[plane] = sweep_base(load_psi(plane), load_psi(plane - 1), load_psi(plane + 1))


def weight_of(k):
    return DELTA * (0.5 if k in (0, NS) else 1.0)


def initial(plane, planes, got_rim, got_mid):
    rim, middle = split(planes)
    value = got_rim[rim.index(plane)] if plane in rim else got_mid[middle.index(plane)]
    return value.astype(jnp.bfloat16)


def other_late_kernel(charges, u, w, psi, wide_core, wide_chip, first_core, first_chip, own_core, own_chip,
                      got_core, got_chip, own_0, own_1, own_2, own_3, own_4, got_rim, got_mid, other_1, other_2,
                      phi, rho, sums, held, other_3):
    side, core = place()
    slope = slopes(charges, side)
    planes, _, lanes = w.shape
    rows = phi.shape[1]
    total = [jnp.zeros((8, lanes), jnp.float32)]
    valence = [charges[jnp.where(side == 0, k, NS - k)].astype(jnp.float32) for k in range(NS + 1)]
    load_w, load_psi = fields_around(core, w, psi, (wide_core, wide_chip))
    load_u = around(core, lambda p: u[p], planes, got_core, got_chip, 0, 3)
    own_first = around(core, None, planes, wide_core, wide_chip, 0, 2)
    other_first = around(core, None, planes, first_core, first_chip, 0, 2)
    own_second = around(core, None, planes, own_core, own_chip, 0, 3)

    def emit(plane, last):
        if 0 <= plane < planes:
            start = (own_0[plane], initial(plane, planes, got_rim, got_mid))
            middle = (own_2[plane], other_2[plane])
        else:
            def back(load, k):
                return (load(plane) / factor(load_w(plane), load_psi(plane), slope[k])).astype(jnp.bfloat16)

            start = (back(own_first, 0), back(other_first, 3))
            middle = (back(own_second, 2), back(load_u, 1))
        own = (start[0], own_1[plane + 1], middle[0], own_3[plane + 1], own_4[plane + 1])
        other = (start[1], other_1[plane + 1], middle[1], other_3[plane + 1], last)
        phi_here = rho_here = 0.0
        for k in range(NS + 1):
            product = own[k].astype(jnp.float32) * other[NS - k].astype(jnp.float32)
            phi_here = phi_here + weight_of(k) * product
            rho_here = rho_here + (weight_of(k) * valence[k]) * product
        rho[plane + 1] = rho_here
        if 0 <= plane < planes:
            kept = phi_here[HALO:HALO + rows]
            phi[plane] = kept
            for row in range(0, rows, 8):
                total[0] = total[0] + kept[row:row + 8]

    late_steps(load_u, load_w, load_psi, planes, slope, (1, 0), held, other_3, emit)
    row = jnp.sum(total[0], 0, keepdims=True)
    row = row[:, :lanes // 2] + row[:, lanes // 2:]
    sums[...] = jnp.broadcast_to(row, sums.shape)


def rim_kernel(psi, wide_core, wide_chip, after, out):
    del after
    _, core = place()
    planes = psi.shape[0]
    load = around(core, lambda p: psi[p], planes, wide_core, wide_chip, 4, 2)
    for at, plane in enumerate((-1, planes)):
        out[at] = sweep_base(load(plane), load(plane - 1), load(plane + 1))


def end_kernel(cells, phi, rho, base, base_rim, sums, density, potential, held):
    planes, rows, _ = phi.shape
    inverse = cells / jnp.sum(sums[...], keepdims=True)
    share = inverse / 7.0
    held[0] = base_rim[0] + rho[0] * share
    held[planes + 1] = base_rim[1] + rho[planes + 1] * share
    for plane in range(planes):
        held[plane + 1] = base[plane] + rho[plane + 1] * share
    for plane in range(planes):
        density[plane] = phi[plane] * inverse
        here = held[plane + 1]
        total = held[plane] + held[plane + 2] + nsum_plane(here)
        value = (total + rho[plane + 1] * inverse - 2.0 * jnp.tanh(0.5 * here) + here) / 7.0
        potential[plane] = value[HALO:HALO + rows]


def body(w_field, psi_init, start_field, charges):
    ends, slabs = lax.axis_size("end"), lax.axis_size("slab")
    count = ends * slabs
    planes, height, lanes = w_field.shape
    rows = height // 2
    wide = rows + 2 * HALO
    swap = [(i, (i + slabs) % count) for i in range(count)]
    by_core = [(i, i ^ 1) for i in range(count)]
    by_chip = []
    for i in range(count):
        at, tile = divmod(i, slabs)
        by_chip.append((i, at * slabs + (tile + (1 if tile % 2 else -1)) % slabs))

    def exchange(pay_core, pay_chip):
        return lax.ppermute(pay_core, AXES, by_core), lax.ppermute(pay_chip, AXES, by_chip)

    def f32(k):
        return sds((k, wide, lanes))

    def bf16(k):
        return sds((k, wide, lanes), jnp.bfloat16)

    def scratch(k):
        return pltpu.VMEM((k, wide, lanes), jnp.float32)

    rim, middle = split(planes)
    (given,) = call(functools.partial(give_kernel, rim), [f32(len(rim))], [start_field], [VMEM], name="give_rim")
    got_rim = lax.ppermute(given, AXES, swap)
    (given,) = call(functools.partial(give_kernel, middle), [f32(len(middle))], [start_field, given], [VMEM, ANY],
                    name="give_middle")
    got_mid = lax.ppermute(given, AXES, swap)
    w, psi, u_own, own_0, *pay = call(
        own_kernel, [f32(planes)] * 3 + [bf16(planes)] + [f32(6)] * 2, [charges, w_field, psi_init, start_field, given],
        [SMEM] + [VMEM] * 3 + [ANY], flops=1e10, name="own")
    fields = exchange(*pay)
    u_rim, *pay = call(
        other_kernel, [f32(len(rim))] + [f32(2)] * 2, [charges, got_rim, w, psi], [SMEM] + [VMEM] * 3, name="other")
    first = exchange(*pay)
    own_1, own_2, u_own, *pay = call(
        own_early_kernel, [bf16(planes + 2), bf16(planes), f32(planes)] + [f32(3)] * 2,
        [charges, u_own, w, psi, *fields, u_rim], [SMEM] + [VMEM] * 5 + [ANY], [scratch(planes + 2)], name="own_early")
    own_edge = exchange(*pay)
    other_1, other_2, u_other, *pay = call(
        other_early_kernel, [bf16(planes + 2), bf16(planes), f32(planes)] + [f32(3)] * 2,
        [charges, u_rim, got_mid, w, psi, *fields, *first], [SMEM] + [VMEM] * 8,
        [scratch(planes + 2), scratch(len(middle))], name="other_early")
    other_edge = exchange(*pay)
    own_3, own_4, base = call(
        own_late_kernel, [bf16(planes + 2)] * 2 + [f32(planes)],
        [charges, u_own, w, psi, *fields, *own_edge, u_other],
        [SMEM] + [VMEM] * 7 + [ANY], [scratch(planes + 4)], name="own_late")
    phi, rho, sums = call(
        other_late_kernel, [sds((planes, rows, lanes)), f32(planes + 2), sds((count, lanes // 2))],
        [charges, u_other, w, psi, *fields, *first, *own_edge, *other_edge,
         own_0, own_1, own_2, own_3, own_4, got_rim, got_mid, other_1, other_2],
        [SMEM] + [VMEM] * 20,
        [scratch(planes + 4), pltpu.VMEM((planes + 2, wide, lanes), jnp.bfloat16)], name="other_late")
    total = lax.all_to_all(sums, AXES, 0, 0, tiled=True)
    (base_rim,) = call(rim_kernel, [f32(2)], [psi, *fields, sums], [VMEM] * 3 + [ANY], name="rim")
    cells = float(slabs * planes * height * lanes)
    return tuple(call(
        functools.partial(end_kernel, cells), [sds((planes, rows, lanes))] * 2,
        [phi, rho, base, base_rim, total], [VMEM] * 5, [scratch(planes + 2)], name="finish"))


def solution(mesh):
    in_specs = (P("slab", None, None), P("slab", None, None), P("end", "slab", None, None), P())
    out_specs = (P("slab", "end", None), P("slab", "end", None))
    return jax.shard_map(body, mesh=mesh, in_specs=in_specs, out_specs=out_specs, check_vma=False)
```

```python
import functools

import jax
import jax.numpy as jnp
from jax import lax
from jax.experimental import pallas as pl
from jax.experimental.pallas import tpu as pltpu
from jax.sharding import PartitionSpec as P

NS = 4
DELTA = 1.0 / NS
MOBILITY = 0.15
HALO = 8
AXES = ("end", "slab")

VMEM = pl.BlockSpec(memory_space=pltpu.VMEM)
ANY = pl.BlockSpec(memory_space=pl.ANY)
SMEM = pl.BlockSpec(memory_space=pltpu.SMEM)


def call(kernel, outs, args, specs, scratch=(), flops=2e9, name=None):
    moved = sum(a.size * a.dtype.itemsize for a in args) + sum(o.size * o.dtype.itemsize for o in outs)
    return pl.pallas_call(
        kernel,
        out_shape=tuple(outs),
        in_specs=specs,
        out_specs=tuple(VMEM for _ in outs),
        scratch_shapes=list(scratch),
        cost_estimate=pl.CostEstimate(flops=int(flops), bytes_accessed=int(moved), transcendentals=0),
        compiler_params=pltpu.CompilerParams(vmem_limit_bytes=16 * 1024 * 1024),
        name=name,
    )(*args)


def sds(shape, dtype=jnp.float32):
    return jax.ShapeDtypeStruct(shape, dtype)


def pick(plane_of, dst, half, height):
    rows = height // 2
    base = pl.multiple_of(rows * half, 8)
    before = pl.multiple_of((height - HALO) - rows * half, 8)
    after = pl.multiple_of(rows - rows * half, 8)
    dst(0, HALO, plane_of(before, HALO))
    dst(HALO, rows, plane_of(base, rows))
    dst(HALO + rows, HALO, plane_of(after, HALO))


def extract(src, index, out, half, height):
    def read(at, n):
        return src[index + (pl.ds(at, n), slice(None))]

    def write(at, n, value):
        out[index[-1], pl.ds(at, n), :] = value

    pick(read, write, half, height)


def slopes(charges, side):
    values = []
    for step in range(NS):
        at = jnp.where(side == 0, step, NS - 1 - step)
        values.append(0.5 * (charges[at].astype(jnp.float32) + charges[at + 1].astype(jnp.float32)))
    return values


def factor(w, psi, slope):
    return jnp.exp(-0.5 * DELTA * (w + slope * psi))


def nsum_plane(value):
    rows, lanes = value.shape
    total = pltpu.roll(value, 1, 0) + pltpu.roll(value, rows - 1, 0)
    return total + pltpu.roll(value, 1, 1) + pltpu.roll(value, lanes - 1, 1)


def advance(before, here, after, scale):
    total = before + after + nsum_plane(here)
    return scale * (here + MOBILITY * (total - 6.0 * here))


def edges(core, planes, width):
    to_core = jnp.where(core == 0, planes - width, 0)
    return to_core, planes - width - to_core


def place():
    return lax.axis_index("end"), lax.rem(lax.axis_index("slab"), 2)


def around(core, load_inside, planes, from_core, from_chip, base, width):
    def load(plane):
        if plane < 0:
            k = base + plane + width
            return jnp.where(core == 0, from_chip[k], from_core[k])
        if plane >= planes:
            k = base + plane - planes
            return jnp.where(core == 0, from_core[k], from_chip[k])
        return load_inside(plane)

    return load


def fields_around(core, w, psi, fields):
    planes = w.shape[0]
    return (around(core, lambda p: w[p], planes, *fields, 2, 1), around(core, lambda p: psi[p], planes, *fields, 3, 1))


def split(planes):
    return [0, 1, planes - 2, planes - 1], list(range(2, planes - 2))


def give_kernel(which, start, *rest):
    out = rest[-1]
    side = lax.axis_index("end")
    for at, plane in enumerate(which):
        def read(row, n):
            return start[0, plane, pl.ds(row, n), :]

        def write(row, n, value):
            out[at, pl.ds(row, n), :] = value

        pick(read, write, 1 - side, start.shape[2])


def own_kernel(charges, w, psi, start, after, w_out, psi_out, u_out, slice_out, pay_core, pay_chip):
    del after
    side, core = place()
    slope = slopes(charges, side)
    planes, height = w.shape[0], w.shape[1]
    for plane in range(planes):
        extract(w, (plane,), w_out, side, height)
        extract(psi, (plane,), psi_out, side, height)
        extract(start, (0, plane), u_out, side, height)
        value = u_out[plane]
        slice_out[plane] = value.astype(jnp.bfloat16)
        u_out[plane] = factor(w_out[plane], psi_out[plane], slope[0]) * value
    for pay, at, edge in zip((pay_core, pay_chip), edges(core, planes, 2), edges(core, planes, 1)):
        pay[0] = u_out[at]
        pay[1] = u_out[at + 1]
        pay[2] = w_out[edge]
        pay[3] = psi_out[edge]


def other_kernel(charges, got_rim, w, psi, u_rim, pay_core, pay_chip):
    side, core = place()
    slope = slopes(charges, side)
    rim, _ = split(w.shape[0])
    for at, plane in enumerate(rim):
        u_rim[at] = factor(w[plane], psi[plane], slope[NS - 1]) * got_rim[at]
    for pay, at in zip((pay_core, pay_chip), edges(core, 4, 2)):
        for k in range(2):
            pay[k] = u_rim[at + k]


def early_steps(load_u, load_w, load_psi, planes, slope, order, held, out_first, out_second, u_out, pays, core):
    for plane in range(-1, planes + 1):
        w_here, psi_here = load_w(plane), load_psi(plane)
        value = advance(load_u(plane - 1), load_u(plane), load_u(plane + 1), factor(w_here, psi_here, slope[order[0]]))
        if 0 <= plane < planes:
            out_first[plane] = value.astype(jnp.bfloat16)
        held[plane + 1] = factor(w_here, psi_here, slope[order[1]]) * value
    for plane in range(planes):
        w_here, psi_here = load_w(plane), load_psi(plane)
        value = advance(held[plane], held[plane + 1], held[plane + 2], factor(w_here, psi_here, slope[order[1]]))
        out_second[plane] = value.astype(jnp.bfloat16)
        u_out[plane] = factor(w_here, psi_here, slope[order[2]]) * value
    for pay, at in zip(pays, edges(core, planes, 2)):
        for k in range(2):
            pay[k] = u_out[at + k]


def sweep_base(here, before, after):
    total = before + after + nsum_plane(here)
    return (total - 2.0 * jnp.tanh(0.5 * here) + here) / 7.0


def own_early_kernel(charges, u, w, psi, wide_core, wide_chip, after, out_1, out_2, u_out, base, pay_core, pay_chip, held):
    del after
    side, core = place()
    planes = w.shape[0]
    fields = (wide_core, wide_chip)
    load_w, load_psi = fields_around(core, w, psi, fields)
    early_steps(around(core, lambda p: u[p], planes, *fields, 0, 2), load_w, load_psi, planes,
                slopes(charges, side), (0, 1, 2), held, out_1, out_2, u_out, (pay_core, pay_chip), core)
    for plane in range(planes):
        base[plane] = sweep_base(load_psi(plane), load_psi(plane - 1), load_psi(plane + 1))
    for pay, edge in zip((pay_core, pay_chip), edges(core, planes, 1)):
        pay[2] = base[edge]


def other_early_kernel(charges, u_rim, got_mid, w, psi, wide_core, wide_chip, got_core, got_chip,
                       out_1, out_2, u_out, pay_core, pay_chip, held, u_mid):
    side, core = place()
    slope = slopes(charges, side)
    planes = w.shape[0]
    rim, middle = split(planes)
    for at, plane in enumerate(middle):
        u_mid[at] = factor(w[plane], psi[plane], slope[NS - 1]) * got_mid[at]

    def inside(plane):
        return u_rim[rim.index(plane)] if plane in rim else u_mid[middle.index(plane)]

    early_steps(around(core, inside, planes, got_core, got_chip, 0, 2),
                *fields_around(core, w, psi, (wide_core, wide_chip)), planes,
                slope, (3, 2, 1), held, out_1, out_2, u_out, (pay_core, pay_chip), core)


def late_steps(load_u, load_w, load_psi, planes, slope, order, held, out_third, emit_last):
    for plane in range(-1, planes + 1):
        w_here, psi_here = load_w(plane), load_psi(plane)
        value = advance(load_u(plane - 1), load_u(plane), load_u(plane + 1), factor(w_here, psi_here, slope[order[0]]))
        if 0 <= plane < planes:
            out_third[plane] = value.astype(jnp.bfloat16)
        held[plane + 1] = factor(w_here, psi_here, slope[order[1]]) * value
    for plane in range(planes):
        value = advance(held[plane], held[plane + 1], held[plane + 2],
                        factor(load_w(plane), load_psi(plane), slope[order[1]]))
        emit_last(plane, value.astype(jnp.bfloat16))


def own_late_kernel(charges, u, w, psi, wide_core, wide_chip, got_core, got_chip, after, out_3, out_4, held):
    del after
    side, core = place()
    planes = w.shape[0]

    def emit(plane, value):
        out_4[plane] = value

    late_steps(around(core, lambda p: u[p], planes, got_core, got_chip, 0, 2),
               *fields_around(core, w, psi, (wide_core, wide_chip)),
               planes, slopes(charges, side), (2, 3), held, out_3, emit)


def weight_of(k):
    return DELTA * (0.5 if k in (0, NS) else 1.0)


def initial(plane, planes, got_rim, got_mid):
    rim, middle = split(planes)
    value = got_rim[rim.index(plane)] if plane in rim else got_mid[middle.index(plane)]
    return value.astype(jnp.bfloat16)


def other_late_kernel(charges, u, w, psi, wide_core, wide_chip, got_core, got_chip,
                      own_0, own_1, own_2, own_3, own_4, got_rim, got_mid, other_1, other_2,
                      phi, rho, sums, pay_core, pay_chip, held, other_3):
    side, core = place()
    planes, _, lanes = w.shape
    rows = phi.shape[1]
    total = [jnp.zeros((8, lanes), jnp.float32)]
    valence = [charges[jnp.where(side == 0, k, NS - k)].astype(jnp.float32) for k in range(NS + 1)]

    def emit(plane, last):
        own = (own_0[plane], own_1[plane], own_2[plane], own_3[plane], own_4[plane])
        other = (initial(plane, planes, got_rim, got_mid), other_1[plane], other_2[plane], other_3[plane], last)
        phi_here = rho_here = 0.0
        for k in range(NS + 1):
            product = own[k].astype(jnp.float32) * other[NS - k].astype(jnp.float32)
            phi_here = phi_here + weight_of(k) * product
            rho_here = rho_here + (weight_of(k) * valence[k]) * product
        rho[plane] = rho_here
        kept = phi_here[HALO:HALO + rows]
        phi[plane] = kept
        for row in range(0, rows, 8):
            total[0] = total[0] + kept[row:row + 8]

    late_steps(around(core, lambda p: u[p], planes, got_core, got_chip, 0, 2),
               *fields_around(core, w, psi, (wide_core, wide_chip)),
               planes, slopes(charges, side), (1, 0), held, other_3, emit)
    row = jnp.sum(total[0], 0, keepdims=True)
    row = row[:, :lanes // 2] + row[:, lanes // 2:]
    sums[...] = jnp.broadcast_to(row, sums.shape)
    for pay, at in zip((pay_core, pay_chip), edges(core, planes, 1)):
        pay[0] = rho[at]


def end_kernel(cells, phi, rho, base, base_core, base_chip, got_core, got_chip, sums, density, potential, held):
    _, core = place()
    planes, rows, _ = phi.shape
    inverse = cells / jnp.sum(sums[...], keepdims=True)
    share = inverse / 7.0
    load_base = around(core, lambda p: base[p], planes, base_core, base_chip, 2, 1)
    load_rho = around(core, lambda p: rho[p], planes, got_core, got_chip, 0, 1)
    for plane in range(-1, planes + 1):
        held[plane + 1] = load_base(plane) + load_rho(plane) * share
    for plane in range(planes):
        density[plane] = phi[plane] * inverse
        here = held[plane + 1]
        total = held[plane] + held[plane + 2] + nsum_plane(here)
        value = (total + rho[plane] * inverse - 2.0 * jnp.tanh(0.5 * here) + here) / 7.0
        potential[plane] = value[HALO:HALO + rows]


def body(w_field, psi_init, start_field, charges):
    ends, slabs = lax.axis_size("end"), lax.axis_size("slab")
    count = ends * slabs
    planes, height, lanes = w_field.shape
    rows = height // 2
    wide = rows + 2 * HALO
    swap = [(i, (i + slabs) % count) for i in range(count)]
    by_core = [(i, i ^ 1) for i in range(count)]
    by_chip = []
    for i in range(count):
        at, tile = divmod(i, slabs)
        by_chip.append((i, at * slabs + (tile + (1 if tile % 2 else -1)) % slabs))

    def exchange(pay_core, pay_chip):
        return lax.ppermute(pay_core, AXES, by_core), lax.ppermute(pay_chip, AXES, by_chip)

    def f32(k):
        return sds((k, wide, lanes))

    def bf16(k):
        return sds((k, wide, lanes), jnp.bfloat16)

    def scratch(k):
        return pltpu.VMEM((k, wide, lanes), jnp.float32)

    rim, middle = split(planes)
    (given,) = call(functools.partial(give_kernel, rim), [f32(len(rim))], [start_field], [VMEM], name="give_rim")
    got_rim = lax.ppermute(given, AXES, swap)
    (given,) = call(functools.partial(give_kernel, middle), [f32(len(middle))], [start_field, given], [VMEM, ANY],
                    name="give_middle")
    got_mid = lax.ppermute(given, AXES, swap)
    w, psi, u_own, own_0, *pay = call(
        own_kernel, [f32(planes)] * 3 + [bf16(planes)] + [f32(4)] * 2, [charges, w_field, psi_init, start_field, given],
        [SMEM] + [VMEM] * 3 + [ANY], flops=1e10, name="own")
    fields = exchange(*pay)
    u_rim, *pay = call(
        other_kernel, [f32(len(rim))] + [f32(2)] * 2, [charges, got_rim, w, psi], [SMEM] + [VMEM] * 3, name="other")
    first = exchange(*pay)
    own_1, own_2, u_own, base, *pay = call(
        own_early_kernel, [bf16(planes)] * 2 + [f32(planes)] * 2 + [f32(3)] * 2,
        [charges, u_own, w, psi, *fields, u_rim], [SMEM] + [VMEM] * 5 + [ANY], [scratch(planes + 2)], name="own_early")
    own_edge = exchange(*pay)
    other_1, other_2, u_other, *pay = call(
        other_early_kernel, [bf16(planes)] * 2 + [f32(planes)] + [f32(2)] * 2,
        [charges, u_rim, got_mid, w, psi, *fields, *first], [SMEM] + [VMEM] * 8,
        [scratch(planes + 2), scratch(len(middle))], name="other_early")
    other_edge = exchange(*pay)
    own_3, own_4 = call(
        own_late_kernel, [bf16(planes)] * 2, [charges, u_own, w, psi, *fields, *own_edge, u_other],
        [SMEM] + [VMEM] * 7 + [ANY], [scratch(planes + 2)], name="own_late")
    phi, rho, sums, *pay = call(
        other_late_kernel, [sds((planes, rows, lanes)), f32(planes), sds((count, lanes // 2))] + [f32(1)] * 2,
        [charges, u_other, w, psi, *fields, *other_edge,
         own_0, own_1, own_2, own_3, own_4, got_rim, got_mid, other_1, other_2],
        [SMEM] + [VMEM] * 16,
        [scratch(planes + 2), pltpu.VMEM((planes, wide, lanes), jnp.bfloat16)], name="other_late")
    total = lax.all_to_all(sums, AXES, 0, 0, tiled=True)
    rho_edge = exchange(*pay)
    cells = float(slabs * planes * height * lanes)
    return tuple(call(
        functools.partial(end_kernel, cells), [sds((planes, rows, lanes))] * 2,
        [phi, rho, base, *own_edge, *rho_edge, total], [VMEM] * 8, [scratch(planes + 2)], name="finish"))


def solution(mesh):
    in_specs = (P("slab", None, None), P("slab", None, None), P("end", "slab", None, None), P())
    out_specs = (P("slab", "end", None), P("slab", "end", None))
    return jax.shard_map(body, mesh=mesh, in_specs=in_specs, out_specs=out_specs, check_vma=False)
```

```python
import functools

import jax
import jax.numpy as jnp
from jax import lax
from jax.experimental import pallas as pl
from jax.experimental.pallas import tpu as pltpu
from jax.sharding import PartitionSpec as P

NS = 4
DELTA = 1.0 / NS
MOBILITY = 0.15
HALO = NS
AXES = ("end", "slab")

VMEM = pl.BlockSpec(memory_space=pltpu.VMEM)
ANY = pl.BlockSpec(memory_space=pl.ANY)
SMEM = pl.BlockSpec(memory_space=pltpu.SMEM)


def call(kernel, outs, args, specs, scratch=(), flops=2e9, name=None):
    moved = sum(a.size * a.dtype.itemsize for a in args) + sum(o.size * o.dtype.itemsize for o in outs)
    return pl.pallas_call(
        kernel,
        out_shape=tuple(outs),
        in_specs=specs,
        out_specs=tuple(VMEM for _ in outs),
        scratch_shapes=list(scratch),
        cost_estimate=pl.CostEstimate(flops=int(flops), bytes_accessed=int(moved), transcendentals=0),
        compiler_params=pltpu.CompilerParams(vmem_limit_bytes=16 * 1024 * 1024),
        name=name,
    )(*args)


def sds(shape, dtype=jnp.float32):
    return jax.ShapeDtypeStruct(shape, dtype)


def window(plane, half):
    height = plane.shape[0]
    rows = height // 2
    turned = pltpu.roll(plane, HALO, 0)
    upper = jnp.concatenate([turned[rows:], turned[:2 * HALO]], 0)
    return jnp.where(half == 0, turned[:rows + 2 * HALO], upper)


def middle_rows(value):
    wide = value.shape[0]
    return pltpu.roll(value, wide - HALO, 0)[:wide - 2 * HALO]


def rounded(value):
    return value.astype(jnp.bfloat16).astype(jnp.float32)


def slopes(charges, side):
    values = []
    for step in range(NS):
        at = jnp.where(side == 0, step, NS - 1 - step)
        values.append(0.5 * (charges[at].astype(jnp.float32) + charges[at + 1].astype(jnp.float32)))
    return values


def factor(w, psi, slope):
    return jnp.exp(-0.5 * DELTA * (w + slope * psi))


def nsum_plane(value):
    rows, lanes = value.shape
    total = pltpu.roll(value, 1, 0) + pltpu.roll(value, rows - 1, 0)
    return total + pltpu.roll(value, 1, 1) + pltpu.roll(value, lanes - 1, 1)


def advance(before, here, after, scale):
    total = before + after + nsum_plane(here)
    return scale * (here + MOBILITY * (total - 6.0 * here))


def edges(core, planes, width):
    to_core = jnp.where(core == 0, planes - width, 0)
    return to_core, planes - width - to_core


def place():
    return lax.axis_index("end"), lax.rem(lax.axis_index("slab"), 2)


def around(core, load_inside, planes, from_core, from_chip, base, width):
    def load(plane):
        if plane < 0:
            k = base + plane + width
            return jnp.where(core == 0, from_chip[k], from_core[k])
        if plane >= planes:
            k = base + plane - planes
            return jnp.where(core == 0, from_core[k], from_chip[k])
        return load_inside(plane)

    return load


def fields_around(core, w, psi, fields):
    planes = w.shape[0]
    return (around(core, lambda p: w[p], planes, *fields, 2, 1), around(core, lambda p: psi[p], planes, *fields, 3, 1))


def split(planes):
    return [0, 1, planes - 2, planes - 1], list(range(2, planes - 2))


def give_kernel(which, start, *rest):
    out = rest[-1]
    side = lax.axis_index("end")
    for at, plane in enumerate(which):
        out[at] = window(start[0, plane], 1 - side)


def own_kernel(charges, w, psi, start, after, w_out, psi_out, u_out, slice_out, pay_core, pay_chip):
    del after
    side, core = place()
    slope = slopes(charges, side)
    planes = w.shape[0]
    for plane in range(planes):
        w_here, psi_here, value = window(w[plane], side), window(psi[plane], side), window(start[0, plane], side)
        w_out[plane] = w_here
        psi_out[plane] = psi_here
        slice_out[plane] = rounded(value)
        u_out[plane] = factor(w_here, psi_here, slope[0]) * value
    for pay, at, edge in zip((pay_core, pay_chip), edges(core, planes, 2), edges(core, planes, 1)):
        pay[0] = u_out[at]
        pay[1] = u_out[at + 1]
        pay[2] = w_out[edge]
        pay[3] = psi_out[edge]


def other_kernel(charges, got_rim, w, psi, u_rim, pay_core, pay_chip):
    side, core = place()
    slope = slopes(charges, side)
    rim, _ = split(w.shape[0])
    for at, plane in enumerate(rim):
        u_rim[at] = factor(w[plane], psi[plane], slope[NS - 1]) * got_rim[at]
    for pay, at in zip((pay_core, pay_chip), edges(core, 4, 2)):
        for k in range(2):
            pay[k] = u_rim[at + k]


def early_steps(load_u, load_w, load_psi, planes, slope, order, held, out_first, out_second, u_out, pays, core):
    for plane in range(-1, planes + 1):
        w_here, psi_here = load_w(plane), load_psi(plane)
        value = advance(load_u(plane - 1), load_u(plane), load_u(plane + 1), factor(w_here, psi_here, slope[order[0]]))
        if 0 <= plane < planes:
            out_first[plane] = rounded(value)
        held[plane + 1] = factor(w_here, psi_here, slope[order[1]]) * value
    for plane in range(planes):
        w_here, psi_here = load_w(plane), load_psi(plane)
        value = advance(held[plane], held[plane + 1], held[plane + 2], factor(w_here, psi_here, slope[order[1]]))
        out_second[plane] = rounded(value)
        u_out[plane] = factor(w_here, psi_here, slope[order[2]]) * value
    for pay, at in zip(pays, edges(core, planes, 2)):
        for k in range(2):
            pay[k] = u_out[at + k]


def sweep_base(here, before, after):
    total = before + after + nsum_plane(here)
    return (total - 2.0 * jnp.tanh(0.5 * here) + here) / 7.0


def own_early_kernel(charges, u, w, psi, wide_core, wide_chip, after, out_1, out_2, u_out, base, pay_core, pay_chip, held):
    del after
    side, core = place()
    planes = w.shape[0]
    fields = (wide_core, wide_chip)
    load_w, load_psi = fields_around(core, w, psi, fields)
    early_steps(around(core, lambda p: u[p], planes, *fields, 0, 2), load_w, load_psi, planes,
                slopes(charges, side), (0, 1, 2), held, out_1, out_2, u_out, (pay_core, pay_chip), core)
    for plane in range(planes):
        base[plane] = sweep_base(load_psi(plane), load_psi(plane - 1), load_psi(plane + 1))
    for pay, edge in zip((pay_core, pay_chip), edges(core, planes, 1)):
        pay[2] = base[edge]


def other_early_kernel(charges, u_rim, got_mid, w, psi, wide_core, wide_chip, got_core, got_chip,
                       out_1, out_2, u_out, pay_core, pay_chip, held, u_mid):
    side, core = place()
    slope = slopes(charges, side)
    planes = w.shape[0]
    rim, middle = split(planes)
    for at, plane in enumerate(middle):
        u_mid[at] = factor(w[plane], psi[plane], slope[NS - 1]) * got_mid[at]

    def inside(plane):
        return u_rim[rim.index(plane)] if plane in rim else u_mid[middle.index(plane)]

    early_steps(around(core, inside, planes, got_core, got_chip, 0, 2),
                *fields_around(core, w, psi, (wide_core, wide_chip)), planes,
                slope, (3, 2, 1), held, out_1, out_2, u_out, (pay_core, pay_chip), core)


def late_steps(load_u, load_w, load_psi, planes, slope, order, held, out_third, emit_last):
    for plane in range(-1, planes + 1):
        w_here, psi_here = load_w(plane), load_psi(plane)
        value = advance(load_u(plane - 1), load_u(plane), load_u(plane + 1), factor(w_here, psi_here, slope[order[0]]))
        if 0 <= plane < planes:
            out_third[plane] = rounded(value)
        held[plane + 1] = factor(w_here, psi_here, slope[order[1]]) * value
    for plane in range(planes):
        value = advance(held[plane], held[plane + 1], held[plane + 2],
                        factor(load_w(plane), load_psi(plane), slope[order[1]]))
        emit_last(plane, rounded(value))


def own_late_kernel(charges, u, w, psi, wide_core, wide_chip, got_core, got_chip, after, out_3, out_4, held):
    del after
    side, core = place()
    planes = w.shape[0]

    def emit(plane, value):
        out_4[plane] = value

    late_steps(around(core, lambda p: u[p], planes, got_core, got_chip, 0, 2),
               *fields_around(core, w, psi, (wide_core, wide_chip)),
               planes, slopes(charges, side), (2, 3), held, out_3, emit)


def weight_of(k):
    return DELTA * (0.5 if k in (0, NS) else 1.0)


def initial(plane, planes, got_rim, got_mid):
    rim, middle = split(planes)
    value = got_rim[rim.index(plane)] if plane in rim else got_mid[middle.index(plane)]
    return rounded(value)


def other_late_kernel(charges, u, w, psi, wide_core, wide_chip, got_core, got_chip,
                      own_0, own_1, own_2, own_3, own_4, got_rim, got_mid, other_1, other_2,
                      phi, rho, sums, pay_core, pay_chip, pay_end, held, other_3):
    side, core = place()
    planes, _, lanes = w.shape
    rows = phi.shape[1]
    total = [jnp.zeros((8, lanes), jnp.float32)]
    valence = [charges[jnp.where(side == 0, k, NS - k)].astype(jnp.float32) for k in range(NS + 1)]

    def emit(plane, last):
        own = (own_0[plane], own_1[plane], own_2[plane], own_3[plane], own_4[plane])
        other = (initial(plane, planes, got_rim, got_mid), other_1[plane], other_2[plane], other_3[plane], last)
        phi_here = rho_here = 0.0
        for k in range(NS + 1):
            product = own[k] * other[NS - k]
            phi_here = phi_here + weight_of(k) * product
            rho_here = rho_here + (weight_of(k) * valence[k]) * product
        rho[plane] = rho_here
        kept = middle_rows(phi_here)
        phi[plane] = kept
        for row in range(0, rows, 8):
            total[0] = total[0] + kept[row:row + 8]

    late_steps(around(core, lambda p: u[p], planes, got_core, got_chip, 0, 2),
               *fields_around(core, w, psi, (wide_core, wide_chip)),
               planes, slopes(charges, side), (1, 0), held, other_3, emit)
    row = jnp.sum(total[0], 0, keepdims=True)
    row = row[:, :lanes // 2] + row[:, lanes // 2:]
    sums[...] = jnp.broadcast_to(row, sums.shape)
    for pay, at in zip((pay_core, pay_chip), edges(core, planes, 1)):
        pay[0] = rho[at]
    row = lax.broadcasted_iota(jnp.int32, (2 * HALO, lanes), 0)
    for plane in range(planes):
        pay_end[plane] = jnp.where(row < HALO, rho[plane, rows:rows + 2 * HALO], rho[plane, :2 * HALO])


def end_kernel(cells, phi, rho, base, base_core, base_chip, got_core, got_chip, got_end, sums, density, potential, held):
    _, core = place()
    planes, rows, _ = phi.shape
    inverse = cells / jnp.sum(sums[...], keepdims=True)
    share = inverse / 7.0
    load_base = around(core, lambda p: base[p], planes, base_core, base_chip, 2, 1)
    load_rho = around(core, lambda p: rho[p], planes, got_core, got_chip, 0, 1)
    for plane in range(-1, planes + 1):
        held[plane + 1] = load_base(plane) + load_rho(plane) * share
    row = lax.broadcasted_iota(jnp.int32, got_end.shape[1:], 0)
    for plane in range(planes):
        for at, mine in ((0, row >= HALO), (rows, row < HALO)):
            part = slice(at, at + 2 * HALO)
            lent = base[plane, part] + got_end[plane] * share
            held[plane + 1, part] = jnp.where(mine, held[plane + 1, part], lent)
    for plane in range(planes):
        density[plane] = phi[plane] * inverse
        here = held[plane + 1]
        total = held[plane] + held[plane + 2] + nsum_plane(here)
        value = (total + rho[plane] * inverse - 2.0 * jnp.tanh(0.5 * here) + here) / 7.0
        potential[plane] = middle_rows(value)


def body(w_field, psi_init, start_field, charges):
    ends, slabs = lax.axis_size("end"), lax.axis_size("slab")
    count = ends * slabs
    planes, height, lanes = w_field.shape
    rows = height // 2
    wide = rows + 2 * HALO
    swap = [(i, (i + slabs) % count) for i in range(count)]
    by_core = [(i, i ^ 1) for i in range(count)]
    by_chip = []
    for i in range(count):
        at, tile = divmod(i, slabs)
        by_chip.append((i, at * slabs + (tile + (1 if tile % 2 else -1)) % slabs))

    def exchange(pay_core, pay_chip):
        return lax.ppermute(pay_core, AXES, by_core), lax.ppermute(pay_chip, AXES, by_chip)

    def f32(k):
        return sds((k, wide, lanes))

    def scratch(k):
        return pltpu.VMEM((k, wide, lanes), jnp.float32)

    rim, middle = split(planes)
    (given,) = call(functools.partial(give_kernel, rim), [f32(len(rim))], [start_field], [VMEM], name="give_rim")
    got_rim = lax.ppermute(given, AXES, swap)
    (given,) = call(functools.partial(give_kernel, middle), [f32(len(middle))], [start_field, given], [VMEM, ANY],
                    name="give_middle")
    got_mid = lax.ppermute(given, AXES, swap)
    w, psi, u_own, own_0, *pay = call(
        own_kernel, [f32(planes)] * 3 + [f32(planes)] + [f32(4)] * 2, [charges, w_field, psi_init, start_field, given],
        [SMEM] + [VMEM] * 3 + [ANY], flops=1e10, name="own")
    fields = exchange(*pay)
    u_rim, *pay = call(
        other_kernel, [f32(len(rim))] + [f32(2)] * 2, [charges, got_rim, w, psi], [SMEM] + [VMEM] * 3, name="other")
    first = exchange(*pay)
    own_1, own_2, u_own, base, *pay = call(
        own_early_kernel, [f32(planes)] * 2 + [f32(planes)] * 2 + [f32(3)] * 2,
        [charges, u_own, w, psi, *fields, u_rim], [SMEM] + [VMEM] * 5 + [ANY], [scratch(planes + 2)], name="own_early")
    own_edge = exchange(*pay)
    other_1, other_2, u_other, *pay = call(
        other_early_kernel, [f32(planes)] * 2 + [f32(planes)] + [f32(2)] * 2,
        [charges, u_rim, got_mid, w, psi, *fields, *first], [SMEM] + [VMEM] * 8,
        [scratch(planes + 2), scratch(len(middle))], name="other_early")
    other_edge = exchange(*pay)
    own_3, own_4 = call(
        own_late_kernel, [f32(planes)] * 2, [charges, u_own, w, psi, *fields, *own_edge, u_other],
        [SMEM] + [VMEM] * 7 + [ANY], [scratch(planes + 2)], name="own_late")
    phi, rho, sums, *pay, pay_end = call(
        other_late_kernel, [sds((planes, rows, lanes)), f32(planes), sds((count, lanes // 2))] + [f32(1)] * 2
        + [sds((planes, 2 * HALO, lanes))],
        [charges, u_other, w, psi, *fields, *other_edge,
         own_0, own_1, own_2, own_3, own_4, got_rim, got_mid, other_1, other_2],
        [SMEM] + [VMEM] * 16,
        [scratch(planes + 2), scratch(planes)], name="other_late")
    total = lax.all_to_all(sums, AXES, 0, 0, tiled=True)
    rho_edge = exchange(*pay)
    rho_end = lax.ppermute(pay_end, AXES, swap)
    cells = float(slabs * planes * height * lanes)
    return tuple(call(
        functools.partial(end_kernel, cells), [sds((planes, rows, lanes))] * 2,
        [phi, rho, base, *own_edge, *rho_edge, rho_end, total], [VMEM] * 9, [scratch(planes + 2)], name="finish"))


def solution(mesh):
    in_specs = (P("slab", None, None), P("slab", None, None), P("end", "slab", None, None), P())
    out_specs = (P("slab", "end", None), P("slab", "end", None))
    return jax.shard_map(body, mesh=mesh, in_specs=in_specs, out_specs=out_specs, check_vma=False)
```

```python
import functools

import jax
import jax.numpy as jnp
from jax import lax
from jax.experimental import pallas as pl
from jax.experimental.pallas import tpu as pltpu
from jax.sharding import PartitionSpec as P

NS = 4
DELTA = 1.0 / NS
MOBILITY = 0.15
HALO = NS
AXES = ("end", "slab")

VMEM = pl.BlockSpec(memory_space=pltpu.VMEM)
ANY = pl.BlockSpec(memory_space=pl.ANY)
SMEM = pl.BlockSpec(memory_space=pltpu.SMEM)


def call(kernel, outs, args, specs, scratch=(), flops=2e9, name=None):
    moved = sum(a.size * a.dtype.itemsize for a in args) + sum(o.size * o.dtype.itemsize for o in outs)
    return pl.pallas_call(
        kernel,
        out_shape=tuple(outs),
        in_specs=specs,
        out_specs=tuple(VMEM for _ in outs),
        scratch_shapes=list(scratch),
        cost_estimate=pl.CostEstimate(flops=int(flops), bytes_accessed=int(moved), transcendentals=0),
        compiler_params=pltpu.CompilerParams(vmem_limit_bytes=16 * 1024 * 1024),
        name=name,
    )(*args)


def sds(shape, dtype=jnp.float32):
    return jax.ShapeDtypeStruct(shape, dtype)


def window(plane, half):
    height = plane.shape[0]
    rows = height // 2
    turned = pltpu.roll(plane, HALO, 0)
    upper = jnp.concatenate([turned[rows:], turned[:2 * HALO]], 0)
    return jnp.where(half == 0, turned[:rows + 2 * HALO], upper)


def middle_rows(value):
    wide = value.shape[0]
    return pltpu.roll(value, wide - HALO, 0)[:wide - 2 * HALO]


def rounded(value):
    return value.astype(jnp.bfloat16).astype(jnp.float32)


def slopes(charges, side):
    values = []
    for step in range(NS):
        at = jnp.where(side == 0, step, NS - 1 - step)
        values.append(0.5 * (charges[at].astype(jnp.float32) + charges[at + 1].astype(jnp.float32)))
    return values


def factor(w, psi, slope):
    return jnp.exp(-0.5 * DELTA * (w + slope * psi))


def nsum_plane(value):
    rows, lanes = value.shape
    total = pltpu.roll(value, 1, 0) + pltpu.roll(value, rows - 1, 0)
    return total + pltpu.roll(value, 1, 1) + pltpu.roll(value, lanes - 1, 1)


def advance(before, here, after, scale):
    total = before + after + nsum_plane(here)
    return scale * (here + MOBILITY * (total - 6.0 * here))


def edges(core, planes, width):
    to_core = jnp.where(core == 0, planes - width, 0)
    return to_core, planes - width - to_core


def place():
    return lax.axis_index("end"), lax.rem(lax.axis_index("slab"), 2)


def around(core, load_inside, planes, from_core, from_chip, base, width):
    def load(plane):
        if plane < 0:
            k = base + plane + width
            return jnp.where(core == 0, from_chip[k], from_core[k])
        if plane >= planes:
            k = base + plane - planes
            return jnp.where(core == 0, from_core[k], from_chip[k])
        return load_inside(plane)

    return load


def split(planes):
    return [0, 1, planes - 2, planes - 1], list(range(2, planes - 2))


def give_kernel(which, start, *rest):
    out = rest[-1]
    side = lax.axis_index("end")
    for at, plane in enumerate(which):
        out[at] = window(start[0, plane], 1 - side)


def own_kernel(charges, w, psi, start, after, w_out, psi_out, u_out, slice_out, pay_core, pay_chip):
    del after
    side, core = place()
    slope = slopes(charges, side)
    planes = w.shape[0]
    for plane in range(planes):
        w_here, psi_here, value = window(w[plane], side), window(psi[plane], side), window(start[0, plane], side)
        w_out[plane] = w_here
        psi_out[plane] = psi_here
        slice_out[plane] = rounded(value)
        u_out[plane] = factor(w_here, psi_here, slope[0]) * value
    for pay, at, edge in zip((pay_core, pay_chip), edges(core, planes, 2), edges(core, planes, 1)):
        pay[0] = u_out[at]
        pay[1] = u_out[at + 1]
        pay[2] = w_out[edge]
        pay[3] = psi_out[edge]


def factor_kernel(charges, w, psi, out):
    slope = slopes(charges, lax.axis_index("end"))
    for plane in range(w.shape[0]):
        for k in range(NS):
            out[k, plane] = factor(w[plane], psi[plane], slope[k])


def factors_around(core, table, charges, side, fields):
    slope = slopes(charges, side)
    planes = table.shape[1]
    load_w = around(core, None, planes, *fields, 2, 1)
    load_psi = around(core, None, planes, *fields, 3, 1)

    def load(plane, k):
        if 0 <= plane < planes:
            return table[k, plane]
        return factor(load_w(plane), load_psi(plane), slope[k])

    return load


def other_kernel(got_rim, table, u_rim, pay_core, pay_chip):
    _, core = place()
    rim, _ = split(table.shape[1])
    for at, plane in enumerate(rim):
        u_rim[at] = table[NS - 1, plane] * got_rim[at]
    for pay, at in zip((pay_core, pay_chip), edges(core, 4, 2)):
        for k in range(2):
            pay[k] = u_rim[at + k]


def early_steps(load_u, scale, planes, order, held, out_first, out_second, u_out, pays, core):
    for plane in range(-1, planes + 1):
        value = advance(load_u(plane - 1), load_u(plane), load_u(plane + 1), scale(plane, order[0]))
        if 0 <= plane < planes:
            out_first[plane] = rounded(value)
        held[plane + 1] = scale(plane, order[1]) * value
    for plane in range(planes):
        value = advance(held[plane], held[plane + 1], held[plane + 2], scale(plane, order[1]))
        out_second[plane] = rounded(value)
        u_out[plane] = scale(plane, order[2]) * value
    for pay, at in zip(pays, edges(core, planes, 2)):
        for k in range(2):
            pay[k] = u_out[at + k]


def sweep_base(here, before, after):
    total = before + after + nsum_plane(here)
    return (total - 2.0 * jnp.tanh(0.5 * here) + here) / 7.0


def own_early_kernel(charges, u, table, psi, wide_core, wide_chip, after, out_1, out_2, u_out, base_rim, pay_core, pay_chip, held):
    del after
    side, core = place()
    planes = psi.shape[0]
    fields = (wide_core, wide_chip)
    early_steps(around(core, lambda p: u[p], planes, *fields, 0, 2), factors_around(core, table, charges, side, fields),
                planes, (0, 1, 2), held, out_1, out_2, u_out, (pay_core, pay_chip), core)
    load_psi = around(core, lambda p: psi[p], planes, *fields, 3, 1)
    for at, plane in enumerate((0, planes - 1)):
        base_rim[at] = sweep_base(load_psi(plane), load_psi(plane - 1), load_psi(plane + 1))
    for pay, edge in zip((pay_core, pay_chip), edges(core, 2, 1)):
        pay[2] = base_rim[edge]


def other_early_kernel(charges, u_rim, got_mid, table, wide_core, wide_chip, got_core, got_chip,
                       out_1, out_2, u_out, pay_core, pay_chip, held, u_mid):
    side, core = place()
    planes = table.shape[1]
    rim, middle = split(planes)
    for at, plane in enumerate(middle):
        u_mid[at] = table[NS - 1, plane] * got_mid[at]

    def inside(plane):
        return u_rim[rim.index(plane)] if plane in rim else u_mid[middle.index(plane)]

    early_steps(around(core, inside, planes, got_core, got_chip, 0, 2),
                factors_around(core, table, charges, side, (wide_core, wide_chip)), planes,
                (3, 2, 1), held, out_1, out_2, u_out, (pay_core, pay_chip), core)


def late_steps(load_u, scale, planes, order, held, out_third, emit_last):
    for plane in range(-1, planes + 1):
        value = advance(load_u(plane - 1), load_u(plane), load_u(plane + 1), scale(plane, order[0]))
        if 0 <= plane < planes:
            out_third[plane] = rounded(value)
        held[plane + 1] = scale(plane, order[1]) * value
    for plane in range(planes):
        value = advance(held[plane], held[plane + 1], held[plane + 2], scale(plane, order[1]))
        emit_last(plane, rounded(value))


def own_late_kernel(charges, u, table, psi, base_rim, wide_core, wide_chip, got_core, got_chip, after, out_3, out_4, base, held):
    del after
    side, core = place()
    planes = psi.shape[0]

    def emit(plane, value):
        out_4[plane] = value

    late_steps(around(core, lambda p: u[p], planes, got_core, got_chip, 0, 2),
               factors_around(core, table, charges, side, (wide_core, wide_chip)),
               planes, (2, 3), held, out_3, emit)
    base[0] = base_rim[0]
    base[planes - 1] = base_rim[1]
    for plane in range(1, planes - 1):
        base[plane] = sweep_base(psi[plane], psi[plane - 1], psi[plane + 1])


def weight_of(k):
    return DELTA * (0.5 if k in (0, NS) else 1.0)


def initial(plane, planes, got_rim, got_mid):
    rim, middle = split(planes)
    value = got_rim[rim.index(plane)] if plane in rim else got_mid[middle.index(plane)]
    return rounded(value)


def other_late_kernel(charges, u, table, wide_core, wide_chip, got_core, got_chip,
                      own_0, own_1, own_2, own_3, own_4, got_rim, got_mid, other_1, other_2,
                      phi, rho, sums, pay_core, pay_chip, pay_end, held, other_3):
    side, core = place()
    planes, rows, lanes = phi.shape
    total = [jnp.zeros((8, lanes), jnp.float32)]
    valence = [charges[jnp.where(side == 0, k, NS - k)].astype(jnp.float32) for k in range(NS + 1)]

    def emit(plane, last):
        own = (own_0[plane], own_1[plane], own_2[plane], own_3[plane], own_4[plane])
        other = (initial(plane, planes, got_rim, got_mid), other_1[plane], other_2[plane], other_3[plane], last)
        phi_here = rho_here = 0.0
        for k in range(NS + 1):
            product = own[k] * other[NS - k]
            phi_here = phi_here + weight_of(k) * product
            rho_here = rho_here + (weight_of(k) * valence[k]) * product
        rho[plane] = rho_here
        kept = middle_rows(phi_here)
        phi[plane] = kept
        for row in range(0, rows, 8):
            total[0] = total[0] + kept[row:row + 8]

    late_steps(around(core, lambda p: u[p], planes, got_core, got_chip, 0, 2),
               factors_around(core, table, charges, side, (wide_core, wide_chip)),
               planes, (1, 0), held, other_3, emit)
    row = jnp.sum(total[0], 0, keepdims=True)
    row = row[:, :lanes // 2] + row[:, lanes // 2:]
    sums[...] = jnp.broadcast_to(row, sums.shape)
    for pay, at in zip((pay_core, pay_chip), edges(core, planes, 1)):
        pay[0] = rho[at]
    row = lax.broadcasted_iota(jnp.int32, (2 * HALO, lanes), 0)
    for plane in range(planes):
        pay_end[plane] = jnp.where(row < HALO, rho[plane, rows:rows + 2 * HALO], rho[plane, :2 * HALO])


def end_kernel(cells, phi, rho, base, base_core, base_chip, got_core, got_chip, got_end, sums, density, potential, held):
    _, core = place()
    planes, rows, _ = phi.shape
    inverse = cells / jnp.sum(sums[...], keepdims=True)
    share = inverse / 7.0
    load_base = around(core, lambda p: base[p], planes, base_core, base_chip, 2, 1)
    load_rho = around(core, lambda p: rho[p], planes, got_core, got_chip, 0, 1)
    for plane in range(-1, planes + 1):
        held[plane + 1] = load_base(plane) + load_rho(plane) * share
    row = lax.broadcasted_iota(jnp.int32, got_end.shape[1:], 0)
    for plane in range(planes):
        for at, mine in ((0, row >= HALO), (rows, row < HALO)):
            part = slice(at, at + 2 * HALO)
            lent = base[plane, part] + got_end[plane] * share
            held[plane + 1, part] = jnp.where(mine, held[plane + 1, part], lent)
    for plane in range(planes):
        density[plane] = phi[plane] * inverse
        here = held[plane + 1]
        total = held[plane] + held[plane + 2] + nsum_plane(here)
        value = (total + rho[plane] * inverse - 2.0 * jnp.tanh(0.5 * here) + here) / 7.0
        potential[plane] = middle_rows(value)


def body(w_field, psi_init, start_field, charges):
    ends, slabs = lax.axis_size("end"), lax.axis_size("slab")
    count = ends * slabs
    planes, height, lanes = w_field.shape
    rows = height // 2
    wide = rows + 2 * HALO
    swap = [(i, (i + slabs) % count) for i in range(count)]
    by_core = [(i, i ^ 1) for i in range(count)]
    by_chip = []
    for i in range(count):
        at, tile = divmod(i, slabs)
        by_chip.append((i, at * slabs + (tile + (1 if tile % 2 else -1)) % slabs))

    def exchange(pay_core, pay_chip):
        return lax.ppermute(pay_core, AXES, by_core), lax.ppermute(pay_chip, AXES, by_chip)

    def f32(k):
        return sds((k, wide, lanes))

    def scratch(k):
        return pltpu.VMEM((k, wide, lanes), jnp.float32)

    rim, middle = split(planes)
    (given,) = call(functools.partial(give_kernel, rim), [f32(len(rim))], [start_field], [VMEM], name="give_rim")
    got_rim = lax.ppermute(given, AXES, swap)
    (given,) = call(functools.partial(give_kernel, middle), [f32(len(middle))], [start_field, given], [VMEM, ANY],
                    name="give_middle")
    got_mid = lax.ppermute(given, AXES, swap)
    w, psi, u_own, own_0, *pay = call(
        own_kernel, [f32(planes)] * 3 + [f32(planes)] + [f32(4)] * 2, [charges, w_field, psi_init, start_field, given],
        [SMEM] + [VMEM] * 3 + [ANY], flops=1e10, name="own")
    fields = exchange(*pay)
    (table,) = call(factor_kernel, [sds((NS, planes, wide, lanes))], [charges, w, psi], [SMEM] + [VMEM] * 2,
                    flops=1e6, name="factors")
    u_rim, *pay = call(
        other_kernel, [f32(len(rim))] + [f32(2)] * 2, [got_rim, table], [VMEM] * 2, name="other")
    first = exchange(*pay)
    own_1, own_2, u_own, base_rim, *pay = call(
        own_early_kernel, [f32(planes)] * 3 + [f32(2)] + [f32(3)] * 2,
        [charges, u_own, table, psi, *fields, u_rim], [SMEM] + [VMEM] * 5 + [ANY], [scratch(planes + 2)], name="own_early")
    own_edge = exchange(*pay)
    other_1, other_2, u_other, *pay = call(
        other_early_kernel, [f32(planes)] * 3 + [f32(2)] * 2,
        [charges, u_rim, got_mid, table, *fields, *first], [SMEM] + [VMEM] * 7,
        [scratch(planes + 2), scratch(len(middle))], name="other_early")
    other_edge = exchange(*pay)
    own_3, own_4, base = call(
        own_late_kernel, [f32(planes)] * 3, [charges, u_own, table, psi, base_rim, *fields, *own_edge, u_other],
        [SMEM] + [VMEM] * 8 + [ANY], [scratch(planes + 2)], name="own_late")
    phi, rho, sums, *pay, pay_end = call(
        other_late_kernel, [sds((planes, rows, lanes)), f32(planes), sds((count, lanes // 2))] + [f32(1)] * 2
        + [sds((planes, 2 * HALO, lanes))],
        [charges, u_other, table, *fields, *other_edge,
         own_0, own_1, own_2, own_3, own_4, got_rim, got_mid, other_1, other_2],
        [SMEM] + [VMEM] * 15,
        [scratch(planes + 2), scratch(planes)], name="other_late")
    total = lax.all_to_all(sums, AXES, 0, 0, tiled=True)
    rho_edge = exchange(*pay)
    rho_end = lax.ppermute(pay_end, AXES, swap)
    cells = float(slabs * planes * height * lanes)
    return tuple(call(
        functools.partial(end_kernel, cells), [sds((planes, rows, lanes))] * 2,
        [phi, rho, base, *own_edge, *rho_edge, rho_end, total], [VMEM] * 9, [scratch(planes + 2)], name="finish"))


def solution(mesh):
    in_specs = (P("slab", None, None), P("slab", None, None), P("end", "slab", None, None), P())
    out_specs = (P("slab", "end", None), P("slab", "end", None))
    return jax.shard_map(body, mesh=mesh, in_specs=in_specs, out_specs=out_specs, check_vma=False)
```

```python
import functools

import jax
import jax.numpy as jnp
from jax import lax
from jax.experimental import pallas as pl
from jax.experimental.pallas import tpu as pltpu
from jax.sharding import PartitionSpec as P

NS = 4
DELTA = 1.0 / NS
MOBILITY = 0.15
HALO = NS
AXES = ("end", "slab")

VMEM = pl.BlockSpec(memory_space=pltpu.VMEM)
ANY = pl.BlockSpec(memory_space=pl.ANY)
SMEM = pl.BlockSpec(memory_space=pltpu.SMEM)


def call(kernel, outs, args, specs, scratch=(), flops=2e9, name=None):
    moved = sum(a.size * a.dtype.itemsize for a in args) + sum(o.size * o.dtype.itemsize for o in outs)
    return pl.pallas_call(
        kernel,
        out_shape=tuple(outs),
        in_specs=specs,
        out_specs=tuple(VMEM for _ in outs),
        scratch_shapes=list(scratch),
        cost_estimate=pl.CostEstimate(flops=int(flops), bytes_accessed=int(moved), transcendentals=0),
        compiler_params=pltpu.CompilerParams(vmem_limit_bytes=16 * 1024 * 1024),
        name=name,
    )(*args)


def sds(shape, dtype=jnp.float32):
    return jax.ShapeDtypeStruct(shape, dtype)


def window(plane, half):
    height = plane.shape[0]
    rows = height // 2
    turned = pltpu.roll(plane, HALO, 0)
    upper = jnp.concatenate([turned[rows:], turned[:2 * HALO]], 0)
    return jnp.where(half == 0, turned[:rows + 2 * HALO], upper)


def middle_rows(value):
    wide = value.shape[0]
    return pltpu.roll(value, wide - HALO, 0)[:wide - 2 * HALO]


def rounded(value):
    return value.astype(jnp.bfloat16).astype(jnp.float32)


def slopes(charges, side):
    values = []
    for step in range(NS):
        at = jnp.where(side == 0, step, NS - 1 - step)
        values.append(0.5 * (charges[at].astype(jnp.float32) + charges[at + 1].astype(jnp.float32)))
    return values


def factor(w, psi, slope):
    return jnp.exp(-0.5 * DELTA * (w + slope * psi))


def nsum_plane(value):
    rows, lanes = value.shape
    total = pltpu.roll(value, 1, 0) + pltpu.roll(value, rows - 1, 0)
    return total + pltpu.roll(value, 1, 1) + pltpu.roll(value, lanes - 1, 1)


def advance(before, here, after, scale):
    total = before + after + nsum_plane(here)
    return scale * (here + MOBILITY * (total - 6.0 * here))


def edges(core, planes, width):
    to_core = jnp.where(core == 0, planes - width, 0)
    return to_core, planes - width - to_core


def place():
    return lax.axis_index("end"), lax.rem(lax.axis_index("slab"), 2)


def around(core, load_inside, planes, from_core, from_chip, base, width):
    def load(plane):
        if plane < 0:
            k = base + plane + width
            return jnp.where(core == 0, from_chip[k], from_core[k])
        if plane >= planes:
            k = base + plane - planes
            return jnp.where(core == 0, from_core[k], from_chip[k])
        return load_inside(plane)

    return load


def split(planes):
    return [0, 1, planes - 2, planes - 1], list(range(2, planes - 2))


def give_kernel(which, start, *rest):
    out = rest[-1]
    side = lax.axis_index("end")
    for at, plane in enumerate(which):
        out[at] = window(start[0, plane], 1 - side)


def own_kernel(charges, w, psi, start, after, w_out, psi_out, u_out, slice_out, pay_core, pay_chip, pay_cross):
    del after
    side, core = place()
    slope = slopes(charges, side)
    planes = w.shape[0]
    for plane in range(planes):
        w_here, psi_here, value = window(w[plane], side), window(psi[plane], side), window(start[0, plane], side)
        w_out[plane] = w_here
        psi_out[plane] = psi_here
        slice_out[plane] = rounded(value)
        u_out[plane] = factor(w_here, psi_here, slope[0]) * value
    for pay, at, edge in zip((pay_core, pay_chip), edges(core, planes, 2), edges(core, planes, 1)):
        pay[0] = u_out[at]
        pay[1] = u_out[at + 1]
        pay[2] = w_out[edge]
        pay[3] = psi_out[edge]
    _, at = edges(core, planes, 2)
    for k in range(2):
        far = 1 - side
        scale = factor(window(w[at + k], far), window(psi[at + k], far), slope[0])
        pay_cross[k] = scale * window(start[0, at + k], far)


def factor_kernel(charges, w, psi, out):
    slope = slopes(charges, lax.axis_index("end"))
    for plane in range(w.shape[0]):
        for k in range(NS):
            out[k, plane] = factor(w[plane], psi[plane], slope[k])


def factors_around(core, table, charges, side, fields):
    slope = slopes(charges, side)
    planes = table.shape[1]
    load_w = around(core, None, planes, *fields, 2, 1)
    load_psi = around(core, None, planes, *fields, 3, 1)

    def load(plane, k):
        if 0 <= plane < planes:
            return table[k, plane]
        return factor(load_w(plane), load_psi(plane), slope[k])

    return load


def other_kernel(got_rim, table, u_rim, pay_core, pay_chip):
    _, core = place()
    rim, _ = split(table.shape[1])
    for at, plane in enumerate(rim):
        u_rim[at] = table[NS - 1, plane] * got_rim[at]
    for pay, at in zip((pay_core, pay_chip), edges(core, 4, 2)):
        for k in range(2):
            pay[k] = u_rim[at + k]


def early_steps(load_u, scale, planes, order, held, out_first, out_second, u_out, pays, core):
    for plane in range(-1, planes + 1):
        value = advance(load_u(plane - 1), load_u(plane), load_u(plane + 1), scale(plane, order[0]))
        if 0 <= plane < planes:
            out_first[plane] = rounded(value)
        held[plane + 1] = scale(plane, order[1]) * value
    for plane in range(planes):
        value = advance(held[plane], held[plane + 1], held[plane + 2], scale(plane, order[1]))
        out_second[plane] = rounded(value)
        u_out[plane] = scale(plane, order[2]) * value
    for pay, at in zip(pays, edges(core, planes, 2)):
        for k in range(2):
            pay[k] = u_out[at + k]


def sweep_base(here, before, after):
    total = before + after + nsum_plane(here)
    return (total - 2.0 * jnp.tanh(0.5 * here) + here) / 7.0


def own_early_kernel(charges, u, table, psi, wide_core, wide_chip, after, out_1, out_2, u_out, base_rim, pay_core, pay_chip, held):
    del after
    side, core = place()
    planes = psi.shape[0]
    fields = (wide_core, wide_chip)
    early_steps(around(core, lambda p: u[p], planes, *fields, 0, 2), factors_around(core, table, charges, side, fields),
                planes, (0, 1, 2), held, out_1, out_2, u_out, (pay_core, pay_chip), core)
    load_psi = around(core, lambda p: psi[p], planes, *fields, 3, 1)
    for at, plane in enumerate((0, planes - 1)):
        base_rim[at] = sweep_base(load_psi(plane), load_psi(plane - 1), load_psi(plane + 1))
    for pay, edge in zip((pay_core, pay_chip), edges(core, 2, 1)):
        pay[2] = base_rim[edge]


def other_early_kernel(charges, u_rim, got_mid, table, wide_core, wide_chip, got_core, got_chip, got_cross,
                       out_1, out_2, u_out, pay_core, pay_chip, held, u_mid, from_chip):
    side, core = place()
    planes = table.shape[1]
    rim, middle = split(planes)
    for at, plane in enumerate(middle):
        u_mid[at] = table[NS - 1, plane] * got_mid[at]
    for k in range(2):
        from_chip[k] = jnp.where(side == core, got_cross[k], got_chip[k])

    def inside(plane):
        return u_rim[rim.index(plane)] if plane in rim else u_mid[middle.index(plane)]

    early_steps(around(core, inside, planes, got_core, from_chip, 0, 2),
                factors_around(core, table, charges, side, (wide_core, wide_chip)), planes,
                (3, 2, 1), held, out_1, out_2, u_out, (pay_core, pay_chip), core)


def late_steps(load_u, scale, planes, order, held, out_third, emit_last):
    for plane in range(-1, planes + 1):
        value = advance(load_u(plane - 1), load_u(plane), load_u(plane + 1), scale(plane, order[0]))
        if 0 <= plane < planes:
            out_third[plane] = rounded(value)
        held[plane + 1] = scale(plane, order[1]) * value
    for plane in range(planes):
        value = advance(held[plane], held[plane + 1], held[plane + 2], scale(plane, order[1]))
        emit_last(plane, rounded(value))


def own_late_kernel(charges, u, table, psi, base_rim, wide_core, wide_chip, got_core, got_chip, after, out_3, out_4, base, held):
    del after
    side, core = place()
    planes = psi.shape[0]

    def emit(plane, value):
        out_4[plane] = value

    late_steps(around(core, lambda p: u[p], planes, got_core, got_chip, 0, 2),
               factors_around(core, table, charges, side, (wide_core, wide_chip)),
               planes, (2, 3), held, out_3, emit)
    base[0] = base_rim[0]
    base[planes - 1] = base_rim[1]
    for plane in range(1, planes - 1):
        base[plane] = sweep_base(psi[plane], psi[plane - 1], psi[plane + 1])


def weight_of(k):
    return DELTA * (0.5 if k in (0, NS) else 1.0)


def initial(plane, planes, got_rim, got_mid):
    rim, middle = split(planes)
    value = got_rim[rim.index(plane)] if plane in rim else got_mid[middle.index(plane)]
    return rounded(value)


def other_late_kernel(charges, u, table, wide_core, wide_chip, got_core, got_chip,
                      own_0, own_1, own_2, own_3, own_4, got_rim, got_mid, other_1, other_2,
                      phi, rho, sums, pay_core, pay_chip, pay_end, held, other_3):
    side, core = place()
    planes, rows, lanes = phi.shape
    total = [jnp.zeros((8, lanes), jnp.float32)]
    valence = [charges[jnp.where(side == 0, k, NS - k)].astype(jnp.float32) for k in range(NS + 1)]

    def emit(plane, last):
        own = (own_0[plane], own_1[plane], own_2[plane], own_3[plane], own_4[plane])
        other = (initial(plane, planes, got_rim, got_mid), other_1[plane], other_2[plane], other_3[plane], last)
        phi_here = rho_here = 0.0
        for k in range(NS + 1):
            product = own[k] * other[NS - k]
            phi_here = phi_here + weight_of(k) * product
            rho_here = rho_here + (weight_of(k) * valence[k]) * product
        rho[plane] = rho_here
        kept = middle_rows(phi_here)
        phi[plane] = kept
        for row in range(0, rows, 8):
            total[0] = total[0] + kept[row:row + 8]

    late_steps(around(core, lambda p: u[p], planes, got_core, got_chip, 0, 2),
               factors_around(core, table, charges, side, (wide_core, wide_chip)),
               planes, (1, 0), held, other_3, emit)
    row = jnp.sum(total[0], 0, keepdims=True)
    row = row[:, :lanes // 2] + row[:, lanes // 2:]
    sums[...] = jnp.broadcast_to(row, sums.shape)
    for pay, at in zip((pay_core, pay_chip), edges(core, planes, 1)):
        pay[0] = rho[at]
    row = lax.broadcasted_iota(jnp.int32, (2 * HALO, lanes), 0)
    for plane in range(planes):
        pay_end[plane] = jnp.where(row < HALO, rho[plane, rows:rows + 2 * HALO], rho[plane, :2 * HALO])


def end_kernel(cells, phi, rho, base, base_core, base_chip, got_core, got_chip, got_end, sums, density, potential, held):
    _, core = place()
    planes, rows, _ = phi.shape
    inverse = cells / jnp.sum(sums[...], keepdims=True)
    share = inverse / 7.0
    load_base = around(core, lambda p: base[p], planes, base_core, base_chip, 2, 1)
    load_rho = around(core, lambda p: rho[p], planes, got_core, got_chip, 0, 1)
    for plane in range(-1, planes + 1):
        held[plane + 1] = load_base(plane) + load_rho(plane) * share
    row = lax.broadcasted_iota(jnp.int32, got_end.shape[1:], 0)
    for plane in range(planes):
        for at, mine in ((0, row >= HALO), (rows, row < HALO)):
            part = slice(at, at + 2 * HALO)
            lent = base[plane, part] + got_end[plane] * share
            held[plane + 1, part] = jnp.where(mine, held[plane + 1, part], lent)
    for plane in range(planes):
        density[plane] = phi[plane] * inverse
        here = held[plane + 1]
        total = held[plane] + held[plane + 2] + nsum_plane(here)
        value = (total + rho[plane] * inverse - 2.0 * jnp.tanh(0.5 * here) + here) / 7.0
        potential[plane] = middle_rows(value)


def body(w_field, psi_init, start_field, charges):
    ends, slabs = lax.axis_size("end"), lax.axis_size("slab")
    count = ends * slabs
    planes, height, lanes = w_field.shape
    rows = height // 2
    wide = rows + 2 * HALO
    swap = [(i, (i + slabs) % count) for i in range(count)]
    by_core = [(i, i ^ 1) for i in range(count)]
    by_chip = []
    for i in range(count):
        at, tile = divmod(i, slabs)
        by_chip.append((i, at * slabs + (tile + (1 if tile % 2 else -1)) % slabs))

    senders = [(i, j) for i, j in by_chip if i // slabs == i % 2]
    crossing = [(i, (j + slabs) % count) for i, j in senders]
    straight = senders

    def exchange(pay_core, pay_chip):
        return lax.ppermute(pay_core, AXES, by_core), lax.ppermute(pay_chip, AXES, by_chip)

    def f32(k):
        return sds((k, wide, lanes))

    def scratch(k):
        return pltpu.VMEM((k, wide, lanes), jnp.float32)

    rim, middle = split(planes)
    (given,) = call(functools.partial(give_kernel, rim), [f32(len(rim))], [start_field], [VMEM], name="give_rim")
    got_rim = lax.ppermute(given, AXES, swap)
    (given,) = call(functools.partial(give_kernel, middle), [f32(len(middle))], [start_field, given], [VMEM, ANY],
                    name="give_middle")
    got_mid = lax.ppermute(given, AXES, swap)
    w, psi, u_own, own_0, *pay, pay_cross = call(
        own_kernel, [f32(planes)] * 4 + [f32(4)] * 2 + [f32(2)], [charges, w_field, psi_init, start_field, given],
        [SMEM] + [VMEM] * 3 + [ANY], flops=1e10, name="own")
    fields = exchange(*pay)
    (table,) = call(factor_kernel, [sds((NS, planes, wide, lanes))], [charges, w, psi], [SMEM] + [VMEM] * 2,
                    flops=1e6, name="factors")
    cross = lax.ppermute(pay_cross, AXES, crossing)
    u_rim, *pay = call(other_kernel, [f32(len(rim))] + [f32(2)] * 2, [got_rim, table], [VMEM] * 2, name="other")
    first = (lax.ppermute(pay[0], AXES, by_core), lax.ppermute(pay[1], AXES, straight), cross)
    own_1, own_2, u_own, base_rim, *pay = call(
        own_early_kernel, [f32(planes)] * 3 + [f32(2)] + [f32(3)] * 2,
        [charges, u_own, table, psi, *fields, u_rim], [SMEM] + [VMEM] * 5 + [ANY], [scratch(planes + 2)], name="own_early")
    own_edge = exchange(*pay)
    other_1, other_2, u_other, *pay = call(
        other_early_kernel, [f32(planes)] * 3 + [f32(2)] * 2,
        [charges, u_rim, got_mid, table, *fields, *first], [SMEM] + [VMEM] * 8,
        [scratch(planes + 2), scratch(len(middle)), scratch(2)], name="other_early")
    other_edge = exchange(*pay)
    own_3, own_4, base = call(
        own_late_kernel, [f32(planes)] * 3, [charges, u_own, table, psi, base_rim, *fields, *own_edge, u_other],
        [SMEM] + [VMEM] * 8 + [ANY], [scratch(planes + 2)], name="own_late")
    phi, rho, sums, *pay, pay_end = call(
        other_late_kernel, [sds((planes, rows, lanes)), f32(planes), sds((count, lanes // 2))] + [f32(1)] * 2
        + [sds((planes, 2 * HALO, lanes))],
        [charges, u_other, table, *fields, *other_edge,
         own_0, own_1, own_2, own_3, own_4, got_rim, got_mid, other_1, other_2],
        [SMEM] + [VMEM] * 15,
        [scratch(planes + 2), scratch(planes)], name="other_late")
    total = lax.all_to_all(sums, AXES, 0, 0, tiled=True)
    rho_edge = exchange(*pay)
    rho_end = lax.ppermute(pay_end, AXES, swap)
    cells = float(slabs * planes * height * lanes)
    return tuple(call(
        functools.partial(end_kernel, cells), [sds((planes, rows, lanes))] * 2,
        [phi, rho, base, *own_edge, *rho_edge, rho_end, total], [VMEM] * 9, [scratch(planes + 2)], name="finish"))


def solution(mesh):
    in_specs = (P("slab", None, None), P("slab", None, None), P("end", "slab", None, None), P())
    out_specs = (P("slab", "end", None), P("slab", "end", None))
    return jax.shard_map(body, mesh=mesh, in_specs=in_specs, out_specs=out_specs, check_vma=False)
```

```python
import functools

import jax
import jax.numpy as jnp
from jax import lax
from jax.experimental import pallas as pl
from jax.experimental.pallas import tpu as pltpu
from jax.sharding import PartitionSpec as P

NS = 4
DELTA = 1.0 / NS
MOBILITY = 0.15
HALO = NS
AXES = ("end", "slab")

VMEM = pl.BlockSpec(memory_space=pltpu.VMEM)
ANY = pl.BlockSpec(memory_space=pl.ANY)
SMEM = pl.BlockSpec(memory_space=pltpu.SMEM)


def call(kernel, outs, args, specs, scratch=(), flops=2e9, name=None):
    moved = sum(a.size * a.dtype.itemsize for a in args) + sum(o.size * o.dtype.itemsize for o in outs)
    return pl.pallas_call(
        kernel,
        out_shape=tuple(outs),
        in_specs=specs,
        out_specs=tuple(VMEM for _ in outs),
        scratch_shapes=list(scratch),
        cost_estimate=pl.CostEstimate(flops=int(flops), bytes_accessed=int(moved), transcendentals=0),
        compiler_params=pltpu.CompilerParams(vmem_limit_bytes=16 * 1024 * 1024),
        name=name,
    )(*args)


def sds(shape, dtype=jnp.float32):
    return jax.ShapeDtypeStruct(shape, dtype)


def window(plane, half):
    height = plane.shape[0]
    rows = height // 2
    turned = pltpu.roll(plane, HALO, 0)
    upper = jnp.concatenate([turned[rows:], turned[:2 * HALO]], 0)
    return jnp.where(half == 0, turned[:rows + 2 * HALO], upper)


def middle_rows(value):
    wide = value.shape[0]
    return pltpu.roll(value, wide - HALO, 0)[:wide - 2 * HALO]


def rounded(value):
    return value.astype(jnp.bfloat16).astype(jnp.float32)


def slopes(charges, side):
    values = []
    for step in range(NS):
        at = jnp.where(side == 0, step, NS - 1 - step)
        values.append(0.5 * (charges[at].astype(jnp.float32) + charges[at + 1].astype(jnp.float32)))
    return values


def factor(w, psi, slope):
    return jnp.exp(-0.5 * DELTA * (w + slope * psi))


def nsum_plane(value):
    rows, lanes = value.shape
    total = pltpu.roll(value, 1, 0) + pltpu.roll(value, rows - 1, 0)
    return total + pltpu.roll(value, 1, 1) + pltpu.roll(value, lanes - 1, 1)


def advance(before, here, after, scale):
    total = before + after + nsum_plane(here)
    return scale * ((1.0 - 6.0 * MOBILITY) * here + MOBILITY * total)


def edges(core, planes, width):
    to_core = jnp.where(core == 0, planes - width, 0)
    return to_core, planes - width - to_core


def place():
    return lax.axis_index("end"), lax.rem(lax.axis_index("slab"), 2)


def around(core, load_inside, planes, from_core, from_chip, base, width):
    def load(plane):
        if plane < 0:
            k = base + plane + width
            return jnp.where(core == 0, from_chip[k], from_core[k])
        if plane >= planes:
            k = base + plane - planes
            return jnp.where(core == 0, from_core[k], from_chip[k])
        return load_inside(plane)

    return load


def split(planes):
    return [0, 1, planes - 2, planes - 1], list(range(2, planes - 2))


def give_kernel(which, start, *rest):
    out = rest[-1]
    side = lax.axis_index("end")
    for at, plane in enumerate(which):
        out[at] = window(start[0, plane], 1 - side)


def own_kernel(charges, w, psi, start, after, w_out, psi_out, u_out, slice_out, pay_core, pay_chip, pay_cross):
    del after
    side, core = place()
    slope = slopes(charges, side)
    planes = w.shape[0]
    for plane in range(planes):
        w_here, psi_here, value = window(w[plane], side), window(psi[plane], side), window(start[0, plane], side)
        w_out[plane] = w_here
        psi_out[plane] = psi_here
        slice_out[plane] = rounded(value)
        u_out[plane] = factor(w_here, psi_here, slope[0]) * value
    for pay, at, edge in zip((pay_core, pay_chip), edges(core, planes, 2), edges(core, planes, 1)):
        pay[0] = u_out[at]
        pay[1] = u_out[at + 1]
        pay[2] = w_out[edge]
        pay[3] = psi_out[edge]
    _, at = edges(core, planes, 2)
    for k in range(2):
        far = 1 - side
        scale = factor(window(w[at + k], far), window(psi[at + k], far), slope[0])
        pay_cross[k] = scale * window(start[0, at + k], far)


def factor_kernel(charges, w, psi, out):
    slope = slopes(charges, lax.axis_index("end"))
    for plane in range(w.shape[0]):
        for k in range(NS):
            out[k, plane] = factor(w[plane], psi[plane], slope[k])


def factors_around(core, table, charges, side, fields):
    slope = slopes(charges, side)
    planes = table.shape[1]
    load_w = around(core, None, planes, *fields, 2, 1)
    load_psi = around(core, None, planes, *fields, 3, 1)

    def load(plane, k):
        if 0 <= plane < planes:
            return table[k, plane]
        return factor(load_w(plane), load_psi(plane), slope[k])

    return load


def other_kernel(got_rim, table, u_rim, pay_core, pay_chip):
    _, core = place()
    rim, _ = split(table.shape[1])
    for at, plane in enumerate(rim):
        u_rim[at] = table[NS - 1, plane] * got_rim[at]
    for pay, at in zip((pay_core, pay_chip), edges(core, 4, 2)):
        for k in range(2):
            pay[k] = u_rim[at + k]


def early_steps(load_u, scale, planes, order, held, out_first, out_second, u_out, pays, core):
    for plane in range(-1, planes + 1):
        value = advance(load_u(plane - 1), load_u(plane), load_u(plane + 1), scale(plane, order[0]))
        if 0 <= plane < planes:
            out_first[plane] = rounded(value)
        held[plane + 1] = scale(plane, order[1]) * value
    for plane in range(planes):
        value = advance(held[plane], held[plane + 1], held[plane + 2], scale(plane, order[1]))
        out_second[plane] = rounded(value)
        u_out[plane] = scale(plane, order[2]) * value
    for pay, at in zip(pays, edges(core, planes, 2)):
        for k in range(2):
            pay[k] = u_out[at + k]


def sweep_base(here, before, after):
    total = before + after + nsum_plane(here)
    return (total - 2.0 * jnp.tanh(0.5 * here) + here) / 7.0


def own_early_kernel(charges, u, table, psi, wide_core, wide_chip, after, out_1, out_2, u_out, base_rim, pay_core, pay_chip, held):
    del after
    side, core = place()
    planes = psi.shape[0]
    fields = (wide_core, wide_chip)
    early_steps(around(core, lambda p: u[p], planes, *fields, 0, 2), factors_around(core, table, charges, side, fields),
                planes, (0, 1, 2), held, out_1, out_2, u_out, (pay_core, pay_chip), core)
    load_psi = around(core, lambda p: psi[p], planes, *fields, 3, 1)
    for at, plane in enumerate((0, planes - 1)):
        base_rim[at] = sweep_base(load_psi(plane), load_psi(plane - 1), load_psi(plane + 1))
    for pay, edge in zip((pay_core, pay_chip), edges(core, 2, 1)):
        pay[2] = base_rim[edge]


def other_early_kernel(charges, got_cross, u_rim, table, wide_core, wide_chip, got_core, got_chip, got_mid,
                       out_1, out_2, u_out, pay_core, pay_chip, held, u_mid, from_chip):
    side, core = place()
    planes = table.shape[1]
    rim, middle = split(planes)
    for at, plane in enumerate(middle):
        u_mid[at] = table[NS - 1, plane] * got_mid[at]
    for k in range(2):
        from_chip[k] = jnp.where(side == core, got_cross[k], got_chip[k])

    def inside(plane):
        return u_rim[rim.index(plane)] if plane in rim else u_mid[middle.index(plane)]

    early_steps(around(core, inside, planes, got_core, from_chip, 0, 2),
                factors_around(core, table, charges, side, (wide_core, wide_chip)), planes,
                (3, 2, 1), held, out_1, out_2, u_out, (pay_core, pay_chip), core)


def late_steps(load_u, scale, planes, order, held, out_third, emit_last):
    for plane in range(-1, planes + 1):
        value = advance(load_u(plane - 1), load_u(plane), load_u(plane + 1), scale(plane, order[0]))
        if 0 <= plane < planes:
            out_third[plane] = rounded(value)
        held[plane + 1] = scale(plane, order[1]) * value
    for plane in range(planes):
        value = advance(held[plane], held[plane + 1], held[plane + 2], scale(plane, order[1]))
        emit_last(plane, rounded(value))


def own_late_kernel(charges, u, table, psi, base_rim, wide_core, wide_chip, got_core, got_chip, after, out_3, out_4, base, held):
    del after
    side, core = place()
    planes = psi.shape[0]

    def emit(plane, value):
        out_4[plane] = value

    late_steps(around(core, lambda p: u[p], planes, got_core, got_chip, 0, 2),
               factors_around(core, table, charges, side, (wide_core, wide_chip)),
               planes, (2, 3), held, out_3, emit)
    base[0] = base_rim[0]
    base[planes - 1] = base_rim[1]
    for plane in range(1, planes - 1):
        base[plane] = sweep_base(psi[plane], psi[plane - 1], psi[plane + 1])


def weight_of(k):
    return DELTA * (0.5 if k in (0, NS) else 1.0)


def initial(plane, planes, got_rim, got_mid):
    rim, middle = split(planes)
    value = got_rim[rim.index(plane)] if plane in rim else got_mid[middle.index(plane)]
    return rounded(value)


def other_late_kernel(charges, u, table, wide_core, wide_chip, got_core, got_chip,
                      own_0, own_1, own_2, own_3, own_4, got_rim, got_mid, other_1, other_2,
                      phi, rho, sums, pay_core, pay_chip, pay_end, held, other_3):
    side, core = place()
    planes, rows, lanes = phi.shape
    total = [jnp.zeros((8, lanes), jnp.float32)]
    valence = [charges[jnp.where(side == 0, k, NS - k)].astype(jnp.float32) for k in range(NS + 1)]

    def emit(plane, last):
        own = (own_0[plane], own_1[plane], own_2[plane], own_3[plane], own_4[plane])
        other = (initial(plane, planes, got_rim, got_mid), other_1[plane], other_2[plane], other_3[plane], last)
        phi_here = rho_here = 0.0
        for k in range(NS + 1):
            product = own[k] * other[NS - k]
            phi_here = phi_here + weight_of(k) * product
            rho_here = rho_here + (weight_of(k) * valence[k]) * product
        rho[plane] = rho_here
        kept = middle_rows(phi_here)
        phi[plane] = kept
        for row in range(0, rows, 8):
            total[0] = total[0] + kept[row:row + 8]

    late_steps(around(core, lambda p: u[p], planes, got_core, got_chip, 0, 2),
               factors_around(core, table, charges, side, (wide_core, wide_chip)),
               planes, (1, 0), held, other_3, emit)
    row = jnp.sum(total[0], 0, keepdims=True)
    row = row[:, :lanes // 2] + row[:, lanes // 2:]
    sums[...] = jnp.broadcast_to(row, sums.shape)
    for pay, at in zip((pay_core, pay_chip), edges(core, planes, 1)):
        pay[0] = rho[at]
    row = lax.broadcasted_iota(jnp.int32, (2 * HALO, lanes), 0)
    for plane in range(planes):
        pay_end[plane] = jnp.where(row < HALO, rho[plane, rows:rows + 2 * HALO], rho[plane, :2 * HALO])


def end_kernel(cells, phi, rho, base, base_core, base_chip, got_core, got_chip, got_end, sums, density, potential, held):
    _, core = place()
    planes, rows, _ = phi.shape
    inverse = cells / jnp.sum(sums[...], keepdims=True)
    share = inverse / 7.0
    load_base = around(core, lambda p: base[p], planes, base_core, base_chip, 2, 1)
    load_rho = around(core, lambda p: rho[p], planes, got_core, got_chip, 0, 1)
    for plane in range(-1, planes + 1):
        held[plane + 1] = load_base(plane) + load_rho(plane) * share
    row = lax.broadcasted_iota(jnp.int32, got_end.shape[1:], 0)
    for plane in range(planes):
        for at, mine in ((0, row >= HALO), (rows, row < HALO)):
            part = slice(at, at + 2 * HALO)
            lent = base[plane, part] + got_end[plane] * share
            held[plane + 1, part] = jnp.where(mine, held[plane + 1, part], lent)
    for plane in range(planes):
        density[plane] = phi[plane] * inverse
        here = held[plane + 1]
        total = held[plane] + held[plane + 2] + nsum_plane(here)
        value = (total + rho[plane] * inverse - 2.0 * jnp.tanh(0.5 * here) + here) / 7.0
        potential[plane] = middle_rows(value)


def body(w_field, psi_init, start_field, charges):
    ends, slabs = lax.axis_size("end"), lax.axis_size("slab")
    count = ends * slabs
    planes, height, lanes = w_field.shape
    rows = height // 2
    wide = rows + 2 * HALO
    swap = [(i, (i + slabs) % count) for i in range(count)]
    by_core = [(i, i ^ 1) for i in range(count)]
    by_chip = []
    for i in range(count):
        at, tile = divmod(i, slabs)
        by_chip.append((i, at * slabs + (tile + (1 if tile % 2 else -1)) % slabs))

    senders = [(i, j) for i, j in by_chip if i // slabs == i % 2]
    crossing = [(i, (j + slabs) % count) for i, j in senders]
    straight = senders

    def exchange(pay_core, pay_chip):
        return lax.ppermute(pay_core, AXES, by_core), lax.ppermute(pay_chip, AXES, by_chip)

    def f32(k):
        return sds((k, wide, lanes))

    def scratch(k):
        return pltpu.VMEM((k, wide, lanes), jnp.float32)

    rim, middle = split(planes)
    (given,) = call(functools.partial(give_kernel, rim), [f32(len(rim))], [start_field], [VMEM], name="give_rim")
    got_rim = lax.ppermute(given, AXES, swap)
    (given,) = call(functools.partial(give_kernel, middle), [f32(len(middle))], [start_field, given], [VMEM, ANY],
                    name="give_middle")
    got_mid = lax.ppermute(given, AXES, swap)
    w, psi, u_own, own_0, *pay, pay_cross = call(
        own_kernel, [f32(planes)] * 4 + [f32(4)] * 2 + [f32(2)], [charges, w_field, psi_init, start_field, given],
        [SMEM] + [VMEM] * 3 + [ANY], flops=1e10, name="own")
    fields = exchange(*pay)
    (table,) = call(factor_kernel, [sds((NS, planes, wide, lanes))], [charges, w, psi], [SMEM] + [VMEM] * 2,
                    flops=1e6, name="factors")
    cross = lax.ppermute(pay_cross, AXES, crossing)
    u_rim, *pay = call(other_kernel, [f32(len(rim))] + [f32(2)] * 2, [got_rim, table], [VMEM] * 2, name="other")
    first = (lax.ppermute(pay[0], AXES, by_core), lax.ppermute(pay[1], AXES, straight), cross)
    own_1, own_2, u_own, base_rim, *pay = call(
        own_early_kernel, [f32(planes)] * 3 + [f32(2)] + [f32(3)] * 2,
        [charges, u_own, table, psi, *fields, u_rim], [SMEM] + [VMEM] * 5 + [ANY], [scratch(planes + 2)], name="own_early")
    own_edge = exchange(*pay)
    other_1, other_2, u_other, *pay = call(
        other_early_kernel, [f32(planes)] * 3 + [f32(2)] * 2,
        [charges, cross, u_rim, table, *fields, *first[:2], got_mid], [SMEM] + [VMEM] * 8,
        [scratch(planes + 2), scratch(len(middle)), scratch(2)], name="other_early")
    other_edge = exchange(*pay)
    own_3, own_4, base = call(
        own_late_kernel, [f32(planes)] * 3, [charges, u_own, table, psi, base_rim, *fields, *own_edge, u_other],
        [SMEM] + [VMEM] * 8 + [ANY], [scratch(planes + 2)], name="own_late")
    phi, rho, sums, *pay, pay_end = call(
        other_late_kernel, [sds((planes, rows, lanes)), f32(planes), sds((count, lanes // 2))] + [f32(1)] * 2
        + [sds((planes, 2 * HALO, lanes))],
        [charges, u_other, table, *fields, *other_edge,
         own_0, own_1, own_2, own_3, own_4, got_rim, got_mid, other_1, other_2],
        [SMEM] + [VMEM] * 15,
        [scratch(planes + 2), scratch(planes)], name="other_late")
    total = lax.all_to_all(sums, AXES, 0, 0, tiled=True)
    rho_edge = exchange(*pay)
    rho_end = lax.ppermute(pay_end, AXES, swap)
    cells = float(slabs * planes * height * lanes)
    return tuple(call(
        functools.partial(end_kernel, cells), [sds((planes, rows, lanes))] * 2,
        [phi, rho, base, *own_edge, *rho_edge, rho_end, total], [VMEM] * 9, [scratch(planes + 2)], name="finish"))


def solution(mesh):
    in_specs = (P("slab", None, None), P("slab", None, None), P("end", "slab", None, None), P())
    out_specs = (P("slab", "end", None), P("slab", "end", None))
    return jax.shard_map(body, mesh=mesh, in_specs=in_specs, out_specs=out_specs, check_vma=False)
```

```python
import functools

import jax
import jax.numpy as jnp
from jax import lax
from jax.experimental import pallas as pl
from jax.experimental.pallas import tpu as pltpu
from jax.sharding import PartitionSpec as P

NS = 4
DELTA = 1.0 / NS
MOBILITY = 0.15
HALO = NS
AXES = ("end", "slab")

VMEM = pl.BlockSpec(memory_space=pltpu.VMEM)
ANY = pl.BlockSpec(memory_space=pl.ANY)
SMEM = pl.BlockSpec(memory_space=pltpu.SMEM)


def call(kernel, outs, args, specs, scratch=(), flops=2e9, name=None):
    moved = sum(a.size * a.dtype.itemsize for a in args) + sum(o.size * o.dtype.itemsize for o in outs)
    return pl.pallas_call(
        kernel,
        out_shape=tuple(outs),
        in_specs=specs,
        out_specs=tuple(VMEM for _ in outs),
        scratch_shapes=list(scratch),
        cost_estimate=pl.CostEstimate(flops=int(flops), bytes_accessed=int(moved), transcendentals=0),
        compiler_params=pltpu.CompilerParams(vmem_limit_bytes=16 * 1024 * 1024),
        name=name,
    )(*args)


def sds(shape, dtype=jnp.float32):
    return jax.ShapeDtypeStruct(shape, dtype)


def window(plane, half):
    height = plane.shape[0]
    rows = height // 2
    turned = pltpu.roll(plane, HALO, 0)
    upper = jnp.concatenate([turned[rows:], turned[:2 * HALO]], 0)
    return jnp.where(half == 0, turned[:rows + 2 * HALO], upper)


def middle_rows(value):
    wide = value.shape[0]
    return pltpu.roll(value, wide - HALO, 0)[:wide - 2 * HALO]


def rounded(value):
    return value.astype(jnp.bfloat16).astype(jnp.float32)


def slopes(charges, side):
    values = []
    for step in range(NS):
        at = jnp.where(side == 0, step, NS - 1 - step)
        values.append(0.5 * (charges[at].astype(jnp.float32) + charges[at + 1].astype(jnp.float32)))
    return values


def factor(w, psi, slope):
    return jnp.exp(-0.5 * DELTA * (w + slope * psi))


def nsum_plane(value):
    rows, lanes = value.shape
    total = pltpu.roll(value, 1, 0) + pltpu.roll(value, rows - 1, 0)
    return total + pltpu.roll(value, 1, 1) + pltpu.roll(value, lanes - 1, 1)


def advance(before, here, after, scale):
    total = before + after + nsum_plane(here)
    return scale * ((1.0 - 6.0 * MOBILITY) * here + MOBILITY * total)


def edges(core, planes, width):
    to_core = jnp.where(core == 0, planes - width, 0)
    return to_core, planes - width - to_core


def place():
    return lax.axis_index("end"), lax.rem(lax.axis_index("slab"), 2)


def around(core, load_inside, planes, from_core, from_chip, base, width):
    def load(plane):
        if plane < 0:
            k = base + plane + width
            return jnp.where(core == 0, from_chip[k], from_core[k])
        if plane >= planes:
            k = base + plane - planes
            return jnp.where(core == 0, from_core[k], from_chip[k])
        return load_inside(plane)

    return load


def split(planes):
    return [0, 1, planes - 2, planes - 1], list(range(2, planes - 2))


def give_kernel(which, start, *rest):
    out = rest[-1]
    side = lax.axis_index("end")
    for at, plane in enumerate(which):
        out[at] = window(start[0, plane], 1 - side)


def own_kernel(charges, w, psi, start, after, w_out, psi_out, u_out, slice_out, pay_core, pay_chip, pay_cross):
    del after
    side, core = place()
    slope = slopes(charges, side)
    planes = w.shape[0]
    for plane in range(planes):
        w_here, psi_here, value = window(w[plane], side), window(psi[plane], side), window(start[0, plane], side)
        w_out[plane] = w_here
        psi_out[plane] = psi_here
        slice_out[plane] = rounded(value)
        u_out[plane] = factor(w_here, psi_here, slope[0]) * value
    for pay, at, edge in zip((pay_core, pay_chip), edges(core, planes, 2), edges(core, planes, 1)):
        pay[0] = u_out[at]
        pay[1] = u_out[at + 1]
        pay[2] = w_out[edge]
        pay[3] = psi_out[edge]
    _, at = edges(core, planes, 2)
    for k in range(2):
        far = 1 - side
        scale = factor(window(w[at + k], far), window(psi[at + k], far), slope[0])
        pay_cross[k] = scale * window(start[0, at + k], far)


def factor_kernel(charges, w, psi, out):
    slope = slopes(charges, lax.axis_index("end"))
    for plane in range(w.shape[0]):
        for k in range(NS):
            out[k, plane] = factor(w[plane], psi[plane], slope[k])


def factors_around(core, table, charges, side, fields):
    slope = slopes(charges, side)
    planes = table.shape[1]
    load_w = around(core, None, planes, *fields, 2, 1)
    load_psi = around(core, None, planes, *fields, 3, 1)

    def load(plane, k):
        if 0 <= plane < planes:
            return table[k, plane]
        return factor(load_w(plane), load_psi(plane), slope[k])

    return load


def other_kernel(got_rim, table, u_rim, pay_core, pay_chip):
    _, core = place()
    rim, _ = split(table.shape[1])
    for at, plane in enumerate(rim):
        u_rim[at] = table[NS - 1, plane] * got_rim[at]
    for pay, at in zip((pay_core, pay_chip), edges(core, 4, 2)):
        for k in range(2):
            pay[k] = u_rim[at + k]


def early_steps(load_u, scale, planes, order, held, out_first, out_second, u_out, pays, core):
    for plane in range(-1, planes + 1):
        value = advance(load_u(plane - 1), load_u(plane), load_u(plane + 1), scale(plane, order[0]))
        if 0 <= plane < planes:
            out_first[plane] = rounded(value)
        held[plane + 1] = scale(plane, order[1]) * value
    for plane in range(planes):
        value = advance(held[plane], held[plane + 1], held[plane + 2], scale(plane, order[1]))
        out_second[plane] = rounded(value)
        u_out[plane] = scale(plane, order[2]) * value
    for pay, at in zip(pays, edges(core, planes, 2)):
        for k in range(2):
            pay[k] = u_out[at + k]


def sweep_base(here, before, after):
    total = before + after + nsum_plane(here)
    return (total - 2.0 * jnp.tanh(0.5 * here) + here) / 7.0


def own_early_kernel(charges, u, table, psi, wide_core, wide_chip, after, out_1, out_2, u_out, base_rim, pay_core, pay_chip, held):
    del after
    side, core = place()
    planes = psi.shape[0]
    fields = (wide_core, wide_chip)
    early_steps(around(core, lambda p: u[p], planes, *fields, 0, 2), factors_around(core, table, charges, side, fields),
                planes, (0, 1, 2), held, out_1, out_2, u_out, (pay_core, pay_chip), core)
    load_psi = around(core, lambda p: psi[p], planes, *fields, 3, 1)
    for at, plane in enumerate((0, planes - 1)):
        base_rim[at] = sweep_base(load_psi(plane), load_psi(plane - 1), load_psi(plane + 1))
    for pay, edge in zip((pay_core, pay_chip), edges(core, 2, 1)):
        pay[2] = base_rim[edge]


def other_early_kernel(charges, got_cross, u_rim, table, wide_core, wide_chip, got_core, got_chip, got_mid,
                       out_1, out_2, u_out, pay_core, pay_chip, held, u_mid, from_chip):
    side, core = place()
    planes = table.shape[1]
    rim, middle = split(planes)
    for at, plane in enumerate(middle):
        u_mid[at] = table[NS - 1, plane] * got_mid[at]
    for k in range(2):
        from_chip[k] = jnp.where(side == core, got_cross[k], got_chip[k])

    def inside(plane):
        return u_rim[rim.index(plane)] if plane in rim else u_mid[middle.index(plane)]

    early_steps(around(core, inside, planes, got_core, from_chip, 0, 2),
                factors_around(core, table, charges, side, (wide_core, wide_chip)), planes,
                (3, 2, 1), held, out_1, out_2, u_out, (pay_core, pay_chip), core)


def late_steps(load_u, scale, planes, order, held, out_third, emit_last):
    for plane in range(-1, planes + 1):
        value = advance(load_u(plane - 1), load_u(plane), load_u(plane + 1), scale(plane, order[0]))
        if 0 <= plane < planes:
            out_third[plane] = rounded(value)
        held[plane + 1] = scale(plane, order[1]) * value
    for plane in range(planes):
        value = advance(held[plane], held[plane + 1], held[plane + 2], scale(plane, order[1]))
        emit_last(plane, rounded(value))


def own_late_kernel(charges, u, table, psi, base_rim, wide_core, wide_chip, got_core, got_chip, after, out_3, out_4, base, held):
    del after
    side, core = place()
    planes = psi.shape[0]

    def emit(plane, value):
        out_4[plane] = value

    late_steps(around(core, lambda p: u[p], planes, got_core, got_chip, 0, 2),
               factors_around(core, table, charges, side, (wide_core, wide_chip)),
               planes, (2, 3), held, out_3, emit)
    base[0] = base_rim[0]
    base[planes - 1] = base_rim[1]
    for plane in range(1, planes - 1):
        base[plane] = sweep_base(psi[plane], psi[plane - 1], psi[plane + 1])


def weight_of(k):
    return DELTA * (0.5 if k in (0, NS) else 1.0)


def initial(plane, planes, got_rim, got_mid):
    rim, middle = split(planes)
    value = got_rim[rim.index(plane)] if plane in rim else got_mid[middle.index(plane)]
    return rounded(value)


def other_late_kernel(charges, u, table, wide_core, wide_chip, got_core, got_chip,
                      own_0, own_1, own_2, own_3, own_4, got_rim, got_mid, other_1, other_2,
                      phi, rho, sums, pay_core, pay_chip, pay_end, held, other_3):
    side, core = place()
    planes, rows, lanes = phi.shape
    total = [jnp.zeros((8, lanes), jnp.float32)]
    valence = [charges[jnp.where(side == 0, k, NS - k)].astype(jnp.float32) for k in range(NS + 1)]

    def emit(plane, last):
        own = (own_0[plane], own_1[plane], own_2[plane], own_3[plane], own_4[plane])
        other = (initial(plane, planes, got_rim, got_mid), other_1[plane], other_2[plane], other_3[plane], last)
        parts, rho_here = [0.0, 0.0], 0.0
        for k in range(NS + 1):
            product = own[k] * other[NS - k]
            parts[k in (0, NS)] = parts[k in (0, NS)] + product
            rho_here = rho_here + (weight_of(k) * valence[k]) * product
        phi_here = weight_of(1) * parts[0] + weight_of(0) * parts[1]
        rho[plane] = rho_here
        kept = middle_rows(phi_here)
        phi[plane] = kept
        for row in range(0, rows, 8):
            total[0] = total[0] + kept[row:row + 8]

    late_steps(around(core, lambda p: u[p], planes, got_core, got_chip, 0, 2),
               factors_around(core, table, charges, side, (wide_core, wide_chip)),
               planes, (1, 0), held, other_3, emit)
    row = jnp.sum(total[0], 0, keepdims=True)
    row = row[:, :lanes // 2] + row[:, lanes // 2:]
    sums[...] = jnp.broadcast_to(row, sums.shape)
    for pay, at in zip((pay_core, pay_chip), edges(core, planes, 1)):
        pay[0] = rho[at]
    row = lax.broadcasted_iota(jnp.int32, (2 * HALO, lanes), 0)
    for plane in range(planes):
        pay_end[plane] = jnp.where(row < HALO, rho[plane, rows:rows + 2 * HALO], rho[plane, :2 * HALO])


def end_kernel(cells, phi, rho, base, base_core, base_chip, got_core, got_chip, got_end, sums, density, potential, held):
    _, core = place()
    planes, rows, _ = phi.shape
    inverse = cells / jnp.sum(sums[...], keepdims=True)
    share = inverse / 7.0
    load_base = around(core, lambda p: base[p], planes, base_core, base_chip, 2, 1)
    load_rho = around(core, lambda p: rho[p], planes, got_core, got_chip, 0, 1)
    for plane in range(-1, planes + 1):
        held[plane + 1] = load_base(plane) + load_rho(plane) * share
    row = lax.broadcasted_iota(jnp.int32, got_end.shape[1:], 0)
    for plane in range(planes):
        for at, mine in ((0, row >= HALO), (rows, row < HALO)):
            part = slice(at, at + 2 * HALO)
            lent = base[plane, part] + got_end[plane] * share
            held[plane + 1, part] = jnp.where(mine, held[plane + 1, part], lent)
    for plane in range(planes):
        density[plane] = phi[plane] * inverse
        here = held[plane + 1]
        total = held[plane] + held[plane + 2] + nsum_plane(here)
        value = (total + rho[plane] * inverse - 2.0 * jnp.tanh(0.5 * here) + here) / 7.0
        potential[plane] = middle_rows(value)


def body(w_field, psi_init, start_field, charges):
    ends, slabs = lax.axis_size("end"), lax.axis_size("slab")
    count = ends * slabs
    planes, height, lanes = w_field.shape
    rows = height // 2
    wide = rows + 2 * HALO
    swap = [(i, (i + slabs) % count) for i in range(count)]
    by_core = [(i, i ^ 1) for i in range(count)]
    by_chip = []
    for i in range(count):
        at, tile = divmod(i, slabs)
        by_chip.append((i, at * slabs + (tile + (1 if tile % 2 else -1)) % slabs))

    senders = [(i, j) for i, j in by_chip if i // slabs == i % 2]
    crossing = [(i, (j + slabs) % count) for i, j in senders]
    straight = senders

    def exchange(pay_core, pay_chip):
        return lax.ppermute(pay_core, AXES, by_core), lax.ppermute(pay_chip, AXES, by_chip)

    def f32(k):
        return sds((k, wide, lanes))

    def scratch(k):
        return pltpu.VMEM((k, wide, lanes), jnp.float32)

    rim, middle = split(planes)
    (given,) = call(functools.partial(give_kernel, rim), [f32(len(rim))], [start_field], [VMEM], name="give_rim")
    got_rim = lax.ppermute(given, AXES, swap)
    (given,) = call(functools.partial(give_kernel, middle), [f32(len(middle))], [start_field, given], [VMEM, ANY],
                    name="give_middle")
    got_mid = lax.ppermute(given, AXES, swap)
    w, psi, u_own, own_0, *pay, pay_cross = call(
        own_kernel, [f32(planes)] * 4 + [f32(4)] * 2 + [f32(2)], [charges, w_field, psi_init, start_field, given],
        [SMEM] + [VMEM] * 3 + [ANY], flops=1e10, name="own")
    fields = exchange(*pay)
    (table,) = call(factor_kernel, [sds((NS, planes, wide, lanes))], [charges, w, psi], [SMEM] + [VMEM] * 2,
                    flops=1e6, name="factors")
    cross = lax.ppermute(pay_cross, AXES, crossing)
    u_rim, *pay = call(other_kernel, [f32(len(rim))] + [f32(2)] * 2, [got_rim, table], [VMEM] * 2, name="other")
    first = (lax.ppermute(pay[0], AXES, by_core), lax.ppermute(pay[1], AXES, straight), cross)
    own_1, own_2, u_own, base_rim, *pay = call(
        own_early_kernel, [f32(planes)] * 3 + [f32(2)] + [f32(3)] * 2,
        [charges, u_own, table, psi, *fields, u_rim], [SMEM] + [VMEM] * 5 + [ANY], [scratch(planes + 2)], name="own_early")
    own_edge = exchange(*pay)
    other_1, other_2, u_other, *pay = call(
        other_early_kernel, [f32(planes)] * 3 + [f32(2)] * 2,
        [charges, cross, u_rim, table, *fields, *first[:2], got_mid], [SMEM] + [VMEM] * 8,
        [scratch(planes + 2), scratch(len(middle)), scratch(2)], name="other_early")
    other_edge = exchange(*pay)
    own_3, own_4, base = call(
        own_late_kernel, [f32(planes)] * 3, [charges, u_own, table, psi, base_rim, *fields, *own_edge, u_other],
        [SMEM] + [VMEM] * 8 + [ANY], [scratch(planes + 2)], name="own_late")
    phi, rho, sums, *pay, pay_end = call(
        other_late_kernel, [sds((planes, rows, lanes)), f32(planes), sds((count, lanes // 2))] + [f32(1)] * 2
        + [sds((planes, 2 * HALO, lanes))],
        [charges, u_other, table, *fields, *other_edge,
         own_0, own_1, own_2, own_3, own_4, got_rim, got_mid, other_1, other_2],
        [SMEM] + [VMEM] * 15,
        [scratch(planes + 2), scratch(planes)], name="other_late")
    total = lax.all_to_all(sums, AXES, 0, 0, tiled=True)
    rho_edge = exchange(*pay)
    rho_end = lax.ppermute(pay_end, AXES, swap)
    cells = float(slabs * planes * height * lanes)
    return tuple(call(
        functools.partial(end_kernel, cells), [sds((planes, rows, lanes))] * 2,
        [phi, rho, base, *own_edge, *rho_edge, rho_end, total], [VMEM] * 9, [scratch(planes + 2)], name="finish"))


def solution(mesh):
    in_specs = (P("slab", None, None), P("slab", None, None), P("end", "slab", None, None), P())
    out_specs = (P("slab", "end", None), P("slab", "end", None))
    return jax.shard_map(body, mesh=mesh, in_specs=in_specs, out_specs=out_specs, check_vma=False)
```
